128 devices in a mesh: frames: 2 (over core), rows: 16 (over z, y), heads: 4 (over x).
Axes of the slice: x: 4, y: 4, z: 4, core: 2. Of those that a mesh axis runs over, the one named last changes fastest.
Arguments:
- queries: bfloat16 [2, 16, 2, 128, 5120], P('frames', 'rows', None, 'heads'), may hold values from -8 to 8
- keys: bfloat16 [2, 16, 2, 128, 5120], P('frames', 'rows', None, 'heads'), may hold values from -8 to 8
- values: bfloat16 [2, 16, 2, 128, 5120], P('frames', 'rows', None, 'heads'), may hold values from -6 to 6
- out_grad: bfloat16 [2, 16, 2, 128, 5120], P('frames', 'rows', None, 'heads'), may hold values from -6 to 6
- neighbours: int32 [2, 16, 2, 12], P('frames', 'rows'), may hold values from -1 to 63, as said below
Outputs:
- query_grad: bfloat16 [2, 16, 2, 128, 5120], P('frames', 'rows', None, 'heads')
- key_grad: bfloat16 [2, 16, 2, 128, 5120], P('frames', 'rows', None, 'heads')
- value_grad: bfloat16 [2, 16, 2, 128, 5120], P('frames', 'rows', None, 'heads')
The draws below stay inside these ranges and needn't reach their ends.
Inputs may be any that keep to these rules, and one draw needn't show every extreme that they name: `neighbours`: each query tile lists, each once and in slots of no fixed order, the tiles of a box around it that reaches at most one tile along each of the three tile dimensions, always itself and always the tiles one row tile away, clipped at the grid's bounds; the other slots hold -1. Some query tile lists 12 tiles.
All inputs are finite; a program needn't handle non-finite values.
Results may differ from the reference program's by a relative error of at most 0.012.
Values may be sent and summed in bfloat16 or wider, within the bound.
A program may use at most 320 MiB of HBM per device.

```python
import jax
import jax.numpy as jnp
import numpy as np
from jax import lax

HEADS = 40
HD = 128
TILE = 128
WT = 2
FT = 2
HT = 16
C = 5120
KMAX = 12


def draw_queries(key, part):
    key = jax.random.fold_in(key, 21)
    samples = jnp.clip(jax.random.normal(key, (FT, HT, WT, TILE, HEADS, HD), jnp.float32), -6.0, 6.0)
    return samples.reshape(FT, HT, WT, TILE, HEADS * HD).astype(jnp.bfloat16)


def draw_keys(key, part):
    key = jax.random.fold_in(key, 22)
    samples = jnp.clip(jax.random.normal(key, (FT, HT, WT, TILE, HEADS, HD), jnp.float32), -6.0, 6.0)
    return samples.reshape(FT, HT, WT, TILE, HEADS * HD).astype(jnp.bfloat16)


def draw_neighbours(key, part):
    key = jax.random.fold_in(key, 7)
    grid_shape = (FT, HT, WT)
    frame_pos = lax.broadcasted_iota(jnp.int32, grid_shape, 0)
    row_pos = lax.broadcasted_iota(jnp.int32, grid_shape, 1)
    col_pos = lax.broadcasted_iota(jnp.int32, grid_shape, 2)
    reach_frame = (jax.random.randint(jax.random.fold_in(key, 1), grid_shape, 0, 4) > 0).astype(jnp.int32)
    reach_col = (jax.random.randint(jax.random.fold_in(key, 2), grid_shape, 0, 4) > 0).astype(jnp.int32)
    centre = (frame_pos == min(1, FT - 1)) & (row_pos == min(1, HT - 1)) & (col_pos == min(1, WT - 1))
    reach_frame = jnp.where(centre, 1, reach_frame)
    reach_col = jnp.where(centre, 1, reach_col)
    offsets = np.array([[a, b, c] for a in (-1, 0, 1) for b in (-1, 0, 1) for c in (-1, 0, 1)], dtype=np.int32)
    frame_off = jnp.asarray(offsets[:, 0])
    row_off = jnp.asarray(offsets[:, 1])
    col_off = jnp.asarray(offsets[:, 2])
    target_frame = frame_pos[..., None] + frame_off
    target_row = row_pos[..., None] + row_off
    target_col = col_pos[..., None] + col_off
    inside = (target_frame >= 0) & (target_frame < FT) & (target_row >= 0) & (target_row < HT) & (target_col >= 0) & (target_col < WT)
    within = (jnp.abs(frame_off) <= reach_frame[..., None]) & (jnp.abs(col_off) <= reach_col[..., None])
    usable = inside & within
    tile_ids = (target_frame * HT + target_row) * WT + target_col
    counter = jnp.arange(27, dtype=jnp.int32)
    shuffle = jax.random.randint(jax.random.fold_in(key, 3), (FT, HT, WT, 27), 0, 1024)
    sort_keys = jnp.where(usable, shuffle * 32 + counter, 1048576 + counter)
    ranking = jnp.argsort(sort_keys, axis=-1, stable=True)[..., :KMAX]
    chosen = jnp.take_along_axis(tile_ids, ranking, axis=-1)
    kept = jnp.take_along_axis(usable, ranking, axis=-1)
    return jnp.where(kept, chosen, -1).astype(jnp.int32)


def shard_levels(own_key, extent, shards, smallest, top_value):
    level, own = 1.0, jax.random.fold_in(own_key, 6)
    for position, parts in shards:
        heights = jnp.exp(jax.random.uniform(jax.random.fold_in(own, position), (parts,), jnp.float32, smallest / len(shards), top_value / len(shards)))
        level = level * jnp.repeat(heights, extent[position] // parts).reshape([-1 if axis == position else 1 for axis in range(len(extent))])
    return level


def noise(own_key, shape, spread, reach, cuts=(), kind=jnp.bfloat16):
    values = jax.random.normal(own_key, shape, jnp.float32) * spread
    if len(cuts) > 0:
        values = shard_levels(own_key, shape, cuts, -0.22, 0.18) * values
    return jnp.clip(values, min=-reach, max=reach).astype(kind)


def setup_inputs(seed: int = 0) -> dict:
    key_list = jax.random.split(jax.random.key(seed), 6)
    queries = draw_queries(jax.random.fold_in(key_list[5], 71), 0)
    keys = draw_keys(jax.random.fold_in(key_list[5], 71), 0)
    values = noise(key_list[2], (FT, HT, WT, TILE, C), 1.0, 6.0, ((0, 2), (1, 16), (3, 4)))
    out_grad = noise(key_list[3], (FT, HT, WT, TILE, C), 1.0, 6.0, ((0, 2), (1, 16), (3, 4)))
    neighbours = draw_neighbours(jax.random.fold_in(key_list[5], 71), 0)
    return dict(queries=queries, keys=keys, values=values, out_grad=out_grad, neighbours=neighbours)


def reference(queries, keys, values, out_grad, neighbours):
    tile_total = FT * HT * WT
    score_scale = HD ** -0.5
    query_rows = queries.reshape(tile_total, TILE, HEADS, HD)
    key_rows = keys.reshape(tile_total, TILE, HEADS, HD)
    value_rows = values.reshape(tile_total, TILE, HEADS, HD)
    grad_rows = out_grad.reshape(tile_total, TILE, HEADS, HD)
    slot_table = neighbours.reshape(tile_total, KMAX).astype(jnp.int32)

    def tile_step(carry, inputs):
        key_grads, value_grads = carry
        query_tile, grad_tile, slots = inputs
        usable = slots >= 0
        safe_slots = jnp.where(usable, slots, 0).astype(jnp.int32)
        window_keys = key_rows[safe_slots].astype(jnp.float32)
        window_values = value_rows[safe_slots].astype(jnp.float32)
        query_wide = query_tile.astype(jnp.float32)
        grad_wide = grad_tile.astype(jnp.float32)
        scores = jnp.einsum("thd,sjhd->htsj", query_wide, window_keys, precision=lax.Precision.HIGHEST) * score_scale
        scores = jnp.where(usable[None, None, :, None], scores, -1e30)
        row_peak = jnp.max(scores, axis=(2, 3), keepdims=True)
        weights = jnp.exp(scores - row_peak)
        attention = weights / jnp.sum(weights, axis=(2, 3), keepdims=True)
        attention_low = attention.astype(jnp.bfloat16).astype(jnp.float32)
        recomputed = jnp.einsum("htsj,sjhd->thd", attention_low, window_values, precision=lax.Precision.HIGHEST)
        row_delta = jnp.sum(grad_wide * recomputed, axis=-1)
        prob_grad = jnp.einsum("thd,sjhd->htsj", grad_wide, window_values, precision=lax.Precision.HIGHEST)
        score_grad = (attention * (prob_grad - row_delta.T[:, :, None, None]) * score_scale).astype(jnp.bfloat16).astype(jnp.float32)
        query_grad = jnp.einsum("htsj,sjhd->thd", score_grad, window_keys, precision=lax.Precision.HIGHEST).astype(jnp.bfloat16)
        key_part = jnp.einsum("htsj,thd->sjhd", score_grad, query_wide, precision=lax.Precision.HIGHEST)
        value_part = jnp.einsum("htsj,thd->sjhd", attention_low, grad_wide, precision=lax.Precision.HIGHEST)
        slot_mask = usable[:, None, None, None]
        key_grads = key_grads.at[safe_slots].add(jnp.where(slot_mask, key_part, jnp.float32(0.0)))
        value_grads = value_grads.at[safe_slots].add(jnp.where(slot_mask, value_part, jnp.float32(0.0)))
        return (key_grads, value_grads), query_grad

    initial = (jnp.zeros((tile_total, TILE, HEADS, HD), jnp.float32), jnp.zeros((tile_total, TILE, HEADS, HD), jnp.float32))
    (key_grads, value_grads), query_grads = lax.scan(tile_step, initial, (query_rows, grad_rows, slot_table))
    full_shape = (FT, HT, WT, TILE, HEADS * HD)
    return (query_grads.reshape(full_shape), key_grads.astype(jnp.bfloat16).reshape(full_shape), value_grads.astype(jnp.bfloat16).reshape(full_shape))
```

```python
import functools

import jax
import jax.numpy as jnp
from jax import lax
from jax.experimental import pallas as pl
from jax.experimental.pallas import tpu as pltpu
from jax.sharding import PartitionSpec as P

MESH = pl.DeviceIdType.MESH
HD = 128
TILE = 128
NROWS = 16
LOG2E = 1.4426950408889634
NONE = -1e30
NT = (((1,), (1,)), ((), ()))
NN = (((1,), (0,)), ((), ()))
TN = (((0,), (0,)), ((), ()))


def dot(a, b, dims):
    return lax.dot_general(a, b, dims, preferred_element_type=jnp.float32)


def phase_a(j, p, qg, kv, bias, es, dps, ms, pst):
    scale = LOG2E * HD**-0.5

    def block(i, carry):
        s, f = i // 2, i % 2
        q = qg[s, j, 0, f].reshape(2 * TILE, HD)
        g = qg[s, j, 1, f].reshape(2 * TILE, HD)
        peaks, sums, prods = [], [], []
        for kt in range(4):
            k = kv[j, 0, kt // 2, kt % 2].reshape(TILE, HD)
            v = kv[j, 1, kt // 2, kt % 2].reshape(TILE, HD)
            st = dot(k, q, NT) * scale
            m = jnp.max(st, axis=0, keepdims=True)
            e = jnp.exp2(st - m)
            dp = dot(v, g, NT)
            es[p, i, kt] = e
            dps[p, i, kt] = dp
            mb = m + bias[s, f, kt : kt + 1, :]
            ms[p, i, kt : kt + 1, :] = mb
            peaks.append(mb)
            sums.append(jnp.sum(e, axis=0, keepdims=True))
            prods.append(jnp.sum(e * dp, axis=0, keepdims=True))
        top = functools.reduce(jnp.maximum, peaks)
        ws = [jnp.exp2(mb - top) for mb in peaks]
        pst[j, s, f, 0:1, :] = top
        pst[j, s, f, 1:2, :] = sum(w * l for w, l in zip(ws, sums))
        pst[j, s, f, 2:3, :] = sum(w * d for w, d in zip(ws, prods))
        return carry

    lax.fori_loop(0, 6, block, 0)


def combine(j, pst, prc, fin):
    for f in range(2):
        parts = [pst[j, 1, f], prc[j, 0, f], prc[j, 1, f]]
        top = functools.reduce(jnp.maximum, [x[0:1] for x in parts])
        ws = [jnp.exp2(x[0:1] - top) for x in parts]
        total = sum(w * x[1:2] for w, x in zip(ws, parts))
        prod = sum(w * x[2:3] for w, x in zip(ws, parts))
        fin[j, 1, f, 0:1, :] = top + jnp.log2(total)
        fin[j, 1, f, 1:2, :] = prod / total


def phase_b(j, p, qg, kv, es, dps, ms, fin, dka, dva, dqs, dqf, ost):
    scale = HD**-0.5
    dka[...] = jnp.zeros_like(dka)
    dva[...] = jnp.zeros_like(dva)

    def block(i, carry):
        s, f = i // 2, i % 2
        q = qg[s, j, 0, f].reshape(2 * TILE, HD)
        g = qg[s, j, 1, f].reshape(2 * TILE, HD)
        lse = fin[j, s, f, 0:1, :]
        delta = fin[j, s, f, 1:2, :]
        dq = jnp.zeros((2 * TILE, HD), jnp.float32)
        for kt in range(4):
            k = kv[j, 0, kt // 2, kt % 2].reshape(TILE, HD)
            r = jnp.exp2(ms[p, i, kt : kt + 1, :] - lse)
            prob = es[p, i, kt] * r
            ds = (prob * (dps[p, i, kt] - delta)).astype(jnp.bfloat16)
            dva[kt] += dot(prob.astype(jnp.bfloat16), g, NN)
            dka[kt] += dot(ds, q, NN)
            dq += dot(ds, k, TN)
        dq = dq * scale
        rows = pl.ds(pl.multiple_of(f * 2 * TILE, 2 * TILE), 2 * TILE)
        dqs[j, s, rows] = dq.astype(jnp.bfloat16)

        @pl.when(s == 1)
        def _():
            dqf[j, rows] = dq

        return carry

    lax.fori_loop(0, 6, block, 0)
    ost[j, 1] = (dka[...] * scale).astype(jnp.bfloat16).reshape(ost.shape[2:])
    ost[j, 2] = dva[...].astype(jnp.bfloat16).reshape(ost.shape[2:])


def kernel(nh, q_ref, k_ref, v_ref, g_ref, nb_ref, oq_ref, ok_ref, ov_ref,
           qg, kv, tab, bias, es, dps, ms, pst, prc, fin, dka, dva, dqs, dqr, dqf, ost,
           xin_s, xin_r, halo_s, halo_r, part_s, part_r, fin_s, fin_r, dq_s, dq_r, out_s, out_r,
           tab_s, tab_r, bias_s, bias_r):
    f = lax.axis_index("frames")
    h = lax.axis_index("rows")
    x = lax.axis_index("heads")
    me = x * 2 + f
    up, down = lax.rem(h + NROWS - 1, NROWS), lax.rem(h + 1, NROWS)
    beside = (f, up, x), (f, down, x)

    def member(k):
        other = lax.rem(me + k, 8)
        return other, (other % 2, h, other // 2)

    barrier = pltpu.get_barrier_semaphore()
    for device in [member(k)[1] for k in range(1, 8)] + list(beside):
        pl.semaphore_signal(barrier, inc=1, device_id=device, device_id_type=MESH)
    pl.semaphore_wait(barrier, 9)

    def remote(src, dst, send, recv, device):
        return pltpu.make_async_remote_copy(
            src_ref=src, dst_ref=dst, send_sem=send, recv_sem=recv, device_id=device, device_id_type=MESH
        )

    def await_bytes(ref, sem):
        pltpu.make_async_copy(ref, ref, sem).wait()

    def lanes(owner, j):
        return pl.ds(pl.multiple_of((owner * nh + j) * HD, HD), HD)

    def enter(j):
        for a, (src, dst) in enumerate(((q_ref, qg.at[1, j, 0]), (g_ref, qg.at[1, j, 1]),
                                        (k_ref, kv.at[j, 0]), (v_ref, kv.at[j, 1]))):
            to = dst.at[f, :, x]
            recv = xin_r.at[j, a // 2]
            pltpu.make_async_copy(src.at[0, 0, :, :, lanes(me, j)], to, recv).start()
            for k in range(1, 8):
                other, device = member(k)
                remote(src.at[0, 0, :, :, lanes(other, j)], to, xin_s.at[j, a], recv, device).start()

    def leave(j, a, out):
        to = out.at[0, 0, :, :, lanes(me, j)]
        pltpu.make_async_copy(ost.at[j, a, f, :, x], to, out_r.at[a]).start()
        for k in range(1, 8):
            other, device = member(k)
            remote(ost.at[j, a, other % 2, :, other // 2], to, out_s.at[j, a], out_r.at[a], device).start()

    lax.fori_loop(0, nh, lambda j, c: (enter(j), c)[1], 0)

    for n, dr in enumerate((1, 0, -1)):
        row = h + dr
        inside = jnp.logical_and(row >= 0, row < NROWS)
        for kt in range(4):
            wanted = jnp.where(inside, (kt // 2 * NROWS + row) * 2 + kt % 2, -2)
            for c in range(2):
                found = jnp.where(nb_ref[0, 0, c : c + 1, :] == wanted, 0.0, NONE)
                found = jnp.max(found, axis=-1, keepdims=True)
                tab[n, f, kt : kt + 1, c * TILE : (c + 1) * TILE] = jnp.broadcast_to(found, (1, TILE))
        tab[n, f, 4:8, :] = jnp.zeros((4, 2 * TILE), jnp.float32)
    swap = remote(tab.at[:, f], tab.at[:, f], tab_s, tab_r, (1 - f, h, x))
    swap.start()
    swap.wait()
    bias[1] = tab[1]
    lend = [remote(tab.at[2 * n], bias.at[2 * n], bias_s.at[n], bias_r.at[n], beside[1 - n]) for n in range(2)]
    for copy in lend:
        copy.start()

    def step(t, carry):
        @pl.when(t < nh)
        def _():
            j = t
            await_bytes(qg.at[1, j], xin_r.at[j, 0])
            for n in range(2):
                remote(qg.at[1, j], qg.at[2 * n, j], halo_s.at[n, j], halo_r.at[n, j], beside[1 - n]).start()

        @pl.when(jnp.logical_and(t >= 2, t < nh + 2))
        def _():
            j = t - 2
            for n in range(2):
                await_bytes(prc.at[j, n], part_r.at[n, j])
            combine(j, pst, prc, fin)
            for n in range(2):
                remote(fin.at[j, 1], fin.at[j, 2 * n], fin_s.at[n, j], fin_r.at[n, j], beside[1 - n]).start()

        @pl.when(jnp.logical_and(t >= 1, t < nh + 1))
        def _():
            j = t - 1

            @pl.when(t == 1)
            def _():
                for copy in lend:
                    copy.wait_recv()

            await_bytes(kv.at[j], xin_r.at[j, 1])
            for n in range(2):
                await_bytes(qg.at[2 * n, j], halo_r.at[n, j])
            phase_a(j, j % 2, qg, kv, bias, es, dps, ms, pst)
            for n in range(2):
                remote(pst.at[j, 2 * n], prc.at[j, 1 - n], part_s.at[n, j], part_r.at[1 - n, j], beside[n]).start()

        @pl.when(jnp.logical_and(t >= 2, t < nh + 2))
        def _():
            j = t - 2
            for n in range(2):
                await_bytes(fin.at[j, 2 * n], fin_r.at[n, j])
            phase_b(j, j % 2, qg, kv, es, dps, ms, fin, dka, dva, dqs, dqf, ost)
            for n in range(2):
                remote(dqs.at[j, 2 * n], dqr.at[j, 1 - n], dq_s.at[n, j], dq_r.at[1 - n, j], beside[n]).start()
            leave(j, 1, ok_ref)
            leave(j, 2, ov_ref)

        @pl.when(t >= 3)
        def _():
            j = t - 3
            for n in range(2):
                await_bytes(dqr.at[j, n], dq_r.at[n, j])
            total = dqf[j] + dqr[j, 0].astype(jnp.float32) + dqr[j, 1].astype(jnp.float32)
            ost[j, 0] = total.astype(jnp.bfloat16).reshape(ost.shape[2:])
            leave(j, 0, oq_ref)

        return carry

    lax.fori_loop(0, nh + 3, step, 0)

    for a, out in enumerate((oq_ref, ok_ref, ov_ref)):
        await_bytes(out, out_r.at[a])
    for copy in lend:
        copy.wait_send()

    def settle(j, carry):
        sent = dqs.at[j, 0, pl.ds(0, 7 * TILE // 2)]
        for a in range(4):
            await_bytes(sent, xin_s.at[j, a])
        for a in range(3):
            await_bytes(sent, out_s.at[j, a])
        for n in range(2):
            await_bytes(qg.at[1, j], halo_s.at[n, j])
            await_bytes(prc.at[j, n], part_s.at[n, j])
            await_bytes(prc.at[j, n], fin_s.at[n, j])
            await_bytes(dqr.at[j, n], dq_s.at[n, j])
        return carry

    lax.fori_loop(0, nh, settle, 0)


def local(queries, keys, values, out_grad, neighbours):
    nh = queries.shape[-1] // HD // 8
    tiles = (2, 2, 4, TILE // 4, HD)
    bf, f32 = jnp.bfloat16, jnp.float32
    dma = pltpu.SemaphoreType.DMA
    any_spec = pl.BlockSpec(memory_space=pl.ANY)
    shape = jax.ShapeDtypeStruct(queries.shape, bf)
    products = 5 * 512 * 1536 * HD * nh
    return pl.pallas_call(
        functools.partial(kernel, nh),
        out_shape=(shape, shape, shape),
        in_specs=[any_spec] * 4 + [pl.BlockSpec(memory_space=pltpu.VMEM)],
        out_specs=[any_spec] * 3,
        scratch_shapes=[
            pltpu.VMEM((3, nh, 2) + tiles, bf),
            pltpu.VMEM((nh, 2) + tiles, bf),
            pltpu.VMEM((3, 2, 8, 256), f32),
            pltpu.VMEM((3, 2, 8, 256), f32),
            pltpu.VMEM((2, 6, 4, TILE, 256), f32),
            pltpu.VMEM((2, 6, 4, TILE, 256), f32),
            pltpu.VMEM((2, 6, 8, 256), f32),
            pltpu.VMEM((nh, 3, 2, 8, 256), f32),
            pltpu.VMEM((nh, 2, 2, 8, 256), f32),
            pltpu.VMEM((nh, 3, 2, 8, 256), f32),
            pltpu.VMEM((4, TILE, HD), f32),
            pltpu.VMEM((4, TILE, HD), f32),
            pltpu.VMEM((nh, 3, 512, HD), bf),
            pltpu.VMEM((nh, 2, 512, HD), bf),
            pltpu.VMEM((nh, 512, HD), f32),
            pltpu.VMEM((nh, 3) + tiles, bf),
            dma((nh, 4)), dma((nh, 2)),
            dma((2, nh)), dma((2, nh)),
            dma((2, nh)), dma((2, nh)),
            dma((2, nh)), dma((2, nh)),
            dma((2, nh)), dma((2, nh)),
            dma((nh, 3)), dma((3,)),
            dma(()), dma(()),
            dma((2,)), dma((2,)),
        ],
        compiler_params=pltpu.CompilerParams(
            collective_id=0, has_side_effects=True, vmem_limit_bytes=48 * 1024 * 1024
        ),
        cost_estimate=pl.CostEstimate(
            flops=2 * products, bytes_accessed=7 * 2 * queries.size, transcendentals=512 * 1536 * nh
        ),
        name="window_backward",
    )(queries, keys, values, out_grad, neighbours)


def solution(mesh):
    whole = P("frames", "rows", None, "heads", None)
    return jax.shard_map(
        local,
        mesh=mesh,
        in_specs=(whole, whole, whole, whole, P("frames", "rows", None, None)),
        out_specs=(whole, whole, whole),
        check_vma=False,
    )
```

```python
import functools

import jax
import jax.numpy as jnp
from jax import lax
from jax.experimental import pallas as pl
from jax.experimental.pallas import tpu as pltpu
from jax.sharding import PartitionSpec as P

MESH = pl.DeviceIdType.MESH
HD = 128
TILE = 128
NROWS = 16
LOG2E = 1.4426950408889634
NONE = -1e30
NT = (((1,), (1,)), ((), ()))
NN = (((1,), (0,)), ((), ()))
TN = (((0,), (0,)), ((), ()))


def dot(a, b, dims):
    return lax.dot_general(a, b, dims, preferred_element_type=jnp.float32)


def phase_a(first, last, j, p, qg, kv, bias, es, dps, ms, pst):
    scale = LOG2E * HD**-0.5

    def block(i, carry):
        s, f = i // 2, i % 2
        q = qg[s, j, 0, f].reshape(2 * TILE, HD)
        g = qg[s, j, 1, f].reshape(2 * TILE, HD)
        peaks, sums, prods = [], [], []
        for kt in range(4):
            k = kv[j, 0, kt // 2, kt % 2].reshape(TILE, HD)
            v = kv[j, 1, kt // 2, kt % 2].reshape(TILE, HD)
            st = dot(k, q, NT) * scale
            m = jnp.max(st, axis=0, keepdims=True)
            e = jnp.exp2(st - m)
            dp = dot(v, g, NT)
            es[p, i, kt] = e
            dps[p, i, kt] = dp
            mb = m + bias[s, f, kt : kt + 1, :]
            ms[p, i, kt : kt + 1, :] = mb
            peaks.append(mb)
            sums.append(jnp.sum(e, axis=0, keepdims=True))
            prods.append(jnp.sum(e * dp, axis=0, keepdims=True))
        top = functools.reduce(jnp.maximum, peaks)
        ws = [jnp.exp2(mb - top) for mb in peaks]
        pst[j, s, f, 0:1, :] = top
        pst[j, s, f, 1:2, :] = sum(w * l for w, l in zip(ws, sums))
        pst[j, s, f, 2:3, :] = sum(w * d for w, d in zip(ws, prods))
        return carry

    lax.fori_loop(first, last, block, 0)


def combine(j, pst, prc, fin):
    for f in range(2):
        parts = [pst[j, 1, f], prc[j, 0, f], prc[j, 1, f]]
        top = functools.reduce(jnp.maximum, [x[0:1] for x in parts])
        ws = [jnp.exp2(x[0:1] - top) for x in parts]
        total = sum(w * x[1:2] for w, x in zip(ws, parts))
        prod = sum(w * x[2:3] for w, x in zip(ws, parts))
        fin[j, 1, f, 0:1, :] = top + jnp.log2(total)
        fin[j, 1, f, 1:2, :] = prod / total


def phase_b(first, last, j, p, qg, kv, es, dps, ms, fin, dka, dva, dqs, dqf, ost):
    scale = HD**-0.5
    dka[...] = jnp.zeros_like(dka)
    dva[...] = jnp.zeros_like(dva)

    def block(i, carry):
        s, f = i // 2, i % 2
        q = qg[s, j, 0, f].reshape(2 * TILE, HD)
        g = qg[s, j, 1, f].reshape(2 * TILE, HD)
        lse = fin[j, s, f, 0:1, :]
        delta = fin[j, s, f, 1:2, :]
        dq = jnp.zeros((2 * TILE, HD), jnp.float32)
        for kt in range(4):
            k = kv[j, 0, kt // 2, kt % 2].reshape(TILE, HD)
            r = jnp.exp2(ms[p, i, kt : kt + 1, :] - lse)
            prob = es[p, i, kt] * r
            ds = (prob * (dps[p, i, kt] - delta)).astype(jnp.bfloat16)
            dva[kt] += dot(prob.astype(jnp.bfloat16), g, NN)
            dka[kt] += dot(ds, q, NN)
            dq += dot(ds, k, TN)
        dq = dq * scale
        rows = pl.ds(pl.multiple_of(f * 2 * TILE, 2 * TILE), 2 * TILE)
        dqs[j, s, rows] = dq.astype(jnp.bfloat16)

        @pl.when(s == 1)
        def _():
            dqf[j, rows] = dq

        return carry

    lax.fori_loop(first, last, block, 0)
    ost[j, 1] = (dka[...] * scale).astype(jnp.bfloat16).reshape(ost.shape[2:])
    ost[j, 2] = dva[...].astype(jnp.bfloat16).reshape(ost.shape[2:])


def kernel(nh, q_ref, k_ref, v_ref, g_ref, nb_hbm, oq_ref, ok_ref, ov_ref,
           nb_ref, qg, kv, tab, bias, es, dps, ms, pst, prc, fin, dka, dva, dqs, dqr, dqf, ost,
           xin_s, xin_r, halo_s, halo_r, part_s, part_r, fin_s, fin_r, dq_s, dq_r, out_s, out_r,
           tab_s, tab_r, bias_s, bias_r, nb_s):
    f = lax.axis_index("frames")
    h = lax.axis_index("rows")
    x = lax.axis_index("heads")
    me = x * 2 + f
    beside = (f, jnp.maximum(h - 1, 0), x), (f, jnp.minimum(h + 1, NROWS - 1), x)
    held = h > 0, h < NROWS - 1
    first, last = jnp.where(held[0], 0, 2), jnp.where(held[1], 6, 4)

    def member(k):
        other = lax.rem(me + k, 8)
        return other, (other % 2, h, other // 2)

    near = pltpu.make_async_copy(nb_hbm, nb_ref, nb_s)
    near.start()
    barrier = pltpu.get_barrier_semaphore()
    for k in range(1, 8):
        pl.semaphore_signal(barrier, inc=1, device_id=member(k)[1], device_id_type=MESH)
    for n in range(2):

        @pl.when(held[n])
        def _():
            pl.semaphore_signal(barrier, inc=1, device_id=beside[n], device_id_type=MESH)

    pl.semaphore_wait(barrier, 7 + held[0].astype(jnp.int32) + held[1].astype(jnp.int32))

    def remote(src, dst, send, recv, device):
        return pltpu.make_async_remote_copy(
            src_ref=src, dst_ref=dst, send_sem=send, recv_sem=recv, device_id=device, device_id_type=MESH
        )

    def await_bytes(ref, sem):
        pltpu.make_async_copy(ref, ref, sem).wait()

    def each(action):
        for n in range(2):
            pl.when(held[n])(functools.partial(action, n))

    def lanes(owner, j):
        return pl.ds(pl.multiple_of((owner * nh + j) * HD, HD), HD)

    def enter(j):
        for a, (src, dst) in enumerate(((q_ref, qg.at[1, j, 0]), (g_ref, qg.at[1, j, 1]),
                                        (k_ref, kv.at[j, 0]), (v_ref, kv.at[j, 1]))):
            to = dst.at[f, :, x]
            recv = xin_r.at[j, a // 2]
            pltpu.make_async_copy(src.at[0, 0, :, :, lanes(me, j)], to, recv).start()
            for k in range(1, 8):
                other, device = member(k)
                remote(src.at[0, 0, :, :, lanes(other, j)], to, xin_s.at[j, a], recv, device).start()

    def leave(j, a, out):
        to = out.at[0, 0, :, :, lanes(me, j)]
        pltpu.make_async_copy(ost.at[j, a, f, :, x], to, out_r.at[a]).start()
        for k in range(1, 8):
            other, device = member(k)
            remote(ost.at[j, a, other % 2, :, other // 2], to, out_s.at[j, a], out_r.at[a], device).start()

    def blank(n):
        dqr[:, n] = jnp.zeros_like(dqr[:, n])
        prc[:, n, :, 0:1, :] = jnp.full_like(prc[:, n, :, 0:1, :], NONE)
        prc[:, n, :, 1:8, :] = jnp.zeros_like(prc[:, n, :, 1:8, :])

    lax.fori_loop(0, nh, lambda j, c: (enter(j), c)[1], 0)

    near.wait()
    for n, dr in enumerate((1, 0, -1)):
        row = h + dr
        inside = jnp.logical_and(row >= 0, row < NROWS)
        for kt in range(4):
            wanted = jnp.where(inside, (kt // 2 * NROWS + row) * 2 + kt % 2, -2)
            for c in range(2):
                found = jnp.where(nb_ref[0, 0, c : c + 1, :] == wanted, 0.0, NONE)
                found = jnp.max(found, axis=-1, keepdims=True)
                tab[n, f, kt : kt + 1, c * TILE : (c + 1) * TILE] = jnp.broadcast_to(found, (1, TILE))
        tab[n, f, 4:8, :] = jnp.zeros((4, 2 * TILE), jnp.float32)
    swap = remote(tab.at[:, f], tab.at[:, f], tab_s, tab_r, (1 - f, h, x))
    swap.start()
    swap.wait()
    bias[1] = tab[1]
    lend = [remote(tab.at[2 * n], bias.at[2 * n], bias_s.at[n], bias_r.at[n], beside[1 - n]) for n in range(2)]
    each(lambda n: lend[1 - n].start())

    @pl.when(h == 0)
    def _():
        blank(0)

    @pl.when(h == NROWS - 1)
    def _():
        blank(1)

    def step(t, carry):
        @pl.when(t < nh)
        def _():
            j = t
            await_bytes(qg.at[1, j], xin_r.at[j, 0])
            each(lambda n: remote(qg.at[1, j], qg.at[2 - 2 * n, j], halo_s.at[n, j], halo_r.at[1 - n, j], beside[n]).start())

        @pl.when(jnp.logical_and(t >= 2, t < nh + 2))
        def _():
            j = t - 2
            each(lambda n: await_bytes(prc.at[j, n], part_r.at[n, j]))
            combine(j, pst, prc, fin)
            each(lambda n: remote(fin.at[j, 1], fin.at[j, 2 - 2 * n], fin_s.at[n, j], fin_r.at[1 - n, j], beside[n]).start())

        @pl.when(jnp.logical_and(t >= 1, t < nh + 1))
        def _():
            j = t - 1

            @pl.when(t == 1)
            def _():
                each(lambda n: lend[n].wait_recv())

            await_bytes(kv.at[j], xin_r.at[j, 1])
            each(lambda n: await_bytes(qg.at[2 * n, j], halo_r.at[n, j]))
            phase_a(first, last, j, lax.rem(j, 3), qg, kv, bias, es, dps, ms, pst)
            each(lambda n: remote(pst.at[j, 2 * n], prc.at[j, 1 - n], part_s.at[n, j], part_r.at[1 - n, j], beside[n]).start())

        @pl.when(jnp.logical_and(t >= 3, t < nh + 3))
        def _():
            j = t - 3
            each(lambda n: await_bytes(fin.at[j, 2 * n], fin_r.at[n, j]))
            phase_b(first, last, j, lax.rem(j, 3), qg, kv, es, dps, ms, fin, dka, dva, dqs, dqf, ost)
            each(lambda n: remote(dqs.at[j, 2 * n], dqr.at[j, 1 - n], dq_s.at[n, j], dq_r.at[1 - n, j], beside[n]).start())
            leave(j, 1, ok_ref)
            leave(j, 2, ov_ref)

        @pl.when(t >= 5)
        def _():
            j = t - 5
            each(lambda n: await_bytes(dqr.at[j, n], dq_r.at[n, j]))
            total = dqf[j] + dqr[j, 0].astype(jnp.float32) + dqr[j, 1].astype(jnp.float32)
            ost[j, 0] = total.astype(jnp.bfloat16).reshape(ost.shape[2:])
            leave(j, 0, oq_ref)

        return carry

    lax.fori_loop(0, nh + 5, step, 0)

    for a, out in enumerate((oq_ref, ok_ref, ov_ref)):
        await_bytes(out, out_r.at[a])
    each(lambda n: lend[1 - n].wait_send())

    def settle(j, carry):
        sent = dqs.at[j, 0, pl.ds(0, 7 * TILE // 2)]
        for a in range(4):
            await_bytes(sent, xin_s.at[j, a])
        for a in range(3):
            await_bytes(sent, out_s.at[j, a])

        def lent(n):
            await_bytes(qg.at[1, j], halo_s.at[n, j])
            await_bytes(prc.at[j, n], part_s.at[n, j])
            await_bytes(prc.at[j, n], fin_s.at[n, j])
            await_bytes(dqr.at[j, n], dq_s.at[n, j])

        each(lent)
        return carry

    lax.fori_loop(0, nh, settle, 0)


def hand_over(aq, ak, av, bq, bk, bv, room, into, out):
    ins = [pltpu.make_async_copy(a, room.at[n], into.at[n]) for n, a in enumerate((aq, ak, av))]
    outs = [pltpu.make_async_copy(room.at[n], b, out.at[n]) for n, b in enumerate((bq, bk, bv))]
    for copy in ins:
        copy.start()
    for arrived, copy in zip(ins, outs):
        arrived.wait()
        copy.start()
    for copy in outs:
        copy.wait()


def local(queries, keys, values, out_grad, neighbours):
    nh = queries.shape[-1] // HD // 8
    tiles = (2, 2, 4, TILE // 4, HD)
    bf, f32 = jnp.bfloat16, jnp.float32
    dma = pltpu.SemaphoreType.DMA
    any_spec = pl.BlockSpec(memory_space=pl.ANY)
    shape = jax.ShapeDtypeStruct(queries.shape, bf)
    products = 5 * 512 * 1536 * HD * nh
    grads = pl.pallas_call(
        functools.partial(kernel, nh),
        out_shape=(shape, shape, shape),
        in_specs=[any_spec] * 5,
        out_specs=[any_spec] * 3,
        scratch_shapes=[
            pltpu.VMEM(neighbours.shape, jnp.int32),
            pltpu.VMEM((3, nh, 2) + tiles, bf),
            pltpu.VMEM((nh, 2) + tiles, bf),
            pltpu.VMEM((3, 2, 8, 256), f32),
            pltpu.VMEM((3, 2, 8, 256), f32),
            pltpu.VMEM((3, 6, 4, TILE, 256), f32),
            pltpu.VMEM((3, 6, 4, TILE, 256), f32),
            pltpu.VMEM((3, 6, 8, 256), f32),
            pltpu.VMEM((nh, 3, 2, 8, 256), f32),
            pltpu.VMEM((nh, 2, 2, 8, 256), f32),
            pltpu.VMEM((nh, 3, 2, 8, 256), f32),
            pltpu.VMEM((4, TILE, HD), f32),
            pltpu.VMEM((4, TILE, HD), f32),
            pltpu.VMEM((nh, 3, 512, HD), bf),
            pltpu.VMEM((nh, 2, 512, HD), bf),
            pltpu.VMEM((nh, 512, HD), f32),
            pltpu.VMEM((nh, 3) + tiles, bf),
            dma((nh, 4)), dma((nh, 2)),
            dma((2, nh)), dma((2, nh)),
            dma((2, nh)), dma((2, nh)),
            dma((2, nh)), dma((2, nh)),
            dma((2, nh)), dma((2, nh)),
            dma((nh, 3)), dma((3,)),
            dma(()), dma(()),
            dma((2,)), dma((2,)),
            dma(()),
        ],
        compiler_params=pltpu.CompilerParams(
            collective_id=0, has_side_effects=True, vmem_limit_bytes=60 * 1024 * 1024
        ),
        cost_estimate=pl.CostEstimate(
            flops=2 * products, bytes_accessed=7 * 2 * queries.size, transcendentals=512 * 1536 * nh
        ),
        name="window_backward",
    )(queries, keys, values, out_grad, neighbours)
    return pl.pallas_call(
        hand_over,
        out_shape=(shape, shape, shape),
        in_specs=[any_spec] * 3,
        out_specs=[any_spec] * 3,
        scratch_shapes=[pltpu.VMEM((3,) + queries.shape, bf), dma((3,)), dma((3,))],
        compiler_params=pltpu.CompilerParams(vmem_limit_bytes=60 * 1024 * 1024),
        name="hand_over",
    )(*grads)


def solution(mesh):
    whole = P("frames", "rows", None, "heads", None)
    return jax.shard_map(
        local,
        mesh=mesh,
        in_specs=(whole, whole, whole, whole, P("frames", "rows", None, None)),
        out_specs=(whole, whole, whole),
        check_vma=False,
    )
```

```python
import functools

import jax
import jax.numpy as jnp
from jax import lax
from jax.experimental import pallas as pl
from jax.experimental.pallas import tpu as pltpu
from jax.sharding import PartitionSpec as P

MESH = pl.DeviceIdType.MESH
HD = 128
TILE = 128
NROWS = 16
LOG2E = 1.4426950408889634
NONE = -1e30
NT = (((1,), (1,)), ((), ()))
NN = (((1,), (0,)), ((), ()))
TN = (((0,), (0,)), ((), ()))


def dot(a, b, dims):
    return lax.dot_general(a, b, dims, preferred_element_type=jnp.float32)


def phase_a(s, j, p, qg, kv, bias, es, dps, ms, pst):
    scale = LOG2E * HD**-0.5

    def block(f, carry):
        i = 2 * s + f
        q = qg[s, j, 0, f].reshape(2 * TILE, HD)
        g = qg[s, j, 1, f].reshape(2 * TILE, HD)
        peaks, sums, prods = [], [], []
        for kt in range(4):
            k = kv[j, 0, kt // 2, kt % 2].reshape(TILE, HD)
            v = kv[j, 1, kt // 2, kt % 2].reshape(TILE, HD)
            st = dot(k, q, NT) * scale
            m = jnp.max(st, axis=0, keepdims=True)
            e = jnp.exp2(st - m)
            dp = dot(v, g, NT)
            es[p, i, kt] = e
            dps[p, i, kt] = dp
            mb = m + bias[s, f, kt : kt + 1, :]
            ms[p, i, kt : kt + 1, :] = mb
            peaks.append(mb)
            sums.append(jnp.sum(e, axis=0, keepdims=True))
            prods.append(jnp.sum(e * dp, axis=0, keepdims=True))
        top = functools.reduce(jnp.maximum, peaks)
        ws = [jnp.exp2(mb - top) for mb in peaks]
        pst[j, s, f, 0:1, :] = top
        pst[j, s, f, 1:2, :] = sum(w * l for w, l in zip(ws, sums))
        pst[j, s, f, 2:3, :] = sum(w * d for w, d in zip(ws, prods))
        return carry

    lax.fori_loop(0, 2, block, 0)


def combine(j, pst, prc, fin):
    for f in range(2):
        parts = [pst[j, 1, f], prc[j, 0, f], prc[j, 1, f]]
        top = functools.reduce(jnp.maximum, [x[0:1] for x in parts])
        ws = [jnp.exp2(x[0:1] - top) for x in parts]
        total = sum(w * x[1:2] for w, x in zip(ws, parts))
        prod = sum(w * x[2:3] for w, x in zip(ws, parts))
        fin[j, 1, f, 0:1, :] = top + jnp.log2(total)
        fin[j, 1, f, 1:2, :] = prod / total


def phase_b(s, j, p, qg, kv, es, dps, ms, fin, dka, dva, dqs, dqf):
    scale = HD**-0.5

    def block(f, carry):
        i = 2 * s + f
        q = qg[s, j, 0, f].reshape(2 * TILE, HD)
        g = qg[s, j, 1, f].reshape(2 * TILE, HD)
        lse = fin[j, s, f, 0:1, :]
        delta = fin[j, s, f, 1:2, :]
        dq = jnp.zeros((2 * TILE, HD), jnp.float32)
        for kt in range(4):
            k = kv[j, 0, kt // 2, kt % 2].reshape(TILE, HD)
            r = jnp.exp2(ms[p, i, kt : kt + 1, :] - lse)
            prob = es[p, i, kt] * r
            ds = (prob * (dps[p, i, kt] - delta)).astype(jnp.bfloat16)
            dva[kt] += dot(prob.astype(jnp.bfloat16), g, NN)
            dka[kt] += dot(ds, q, NN)
            dq += dot(ds, k, TN)
        dq = dq * scale
        rows = pl.ds(pl.multiple_of(f * 2 * TILE, 2 * TILE), 2 * TILE)
        if isinstance(s, int):
            dqf[j, rows] = dq
        else:
            dqs[j, s, rows] = dq.astype(jnp.bfloat16)
        return carry

    lax.fori_loop(0, 2, block, 0)


def kernel(nh, q_ref, k_ref, v_ref, g_ref, nb_hbm, oq_ref, ok_ref, ov_ref,
           nb_ref, qg, kv, tab, bias, es, dps, ms, pst, prc, fin, dka, dva, dqs, dqr, dqf, ost,
           xin_s, xin_r, halo_s, halo_r, part_s, part_r, fin_s, fin_r, dq_s, dq_r, out_s, out_r,
           tab_s, tab_r, bias_s, bias_r, nb_s):
    f = lax.axis_index("frames")
    h = lax.axis_index("rows")
    x = lax.axis_index("heads")
    me = x * 2 + f
    beside = (f, jnp.maximum(h - 1, 0), x), (f, jnp.minimum(h + 1, NROWS - 1), x)
    held = h > 0, h < NROWS - 1

    def member(k):
        other = lax.rem(me + k, 8)
        return other, (other % 2, h, other // 2)

    near = pltpu.make_async_copy(nb_hbm, nb_ref, nb_s)
    near.start()
    barrier = pltpu.get_barrier_semaphore()
    for k in range(1, 8):
        pl.semaphore_signal(barrier, inc=1, device_id=member(k)[1], device_id_type=MESH)
    for n in range(2):

        @pl.when(held[n])
        def _():
            pl.semaphore_signal(barrier, inc=1, device_id=beside[n], device_id_type=MESH)

    pl.semaphore_wait(barrier, 7 + held[0].astype(jnp.int32) + held[1].astype(jnp.int32))

    def remote(src, dst, send, recv, device):
        return pltpu.make_async_remote_copy(
            src_ref=src, dst_ref=dst, send_sem=send, recv_sem=recv, device_id=device, device_id_type=MESH
        )

    def await_bytes(ref, sem):
        pltpu.make_async_copy(ref, ref, sem).wait()

    def each(action):
        for n in range(2):
            pl.when(held[n])(functools.partial(action, n))

    def lanes(owner, j):
        return pl.ds(pl.multiple_of((owner * nh + j) * HD, HD), HD)

    def enter(j, pair):
        sides = ((q_ref, qg.at[1, j, 0]), (g_ref, qg.at[1, j, 1])), ((k_ref, kv.at[j, 0]), (v_ref, kv.at[j, 1]))
        for a, (src, dst) in enumerate(sides[pair]):
            to = dst.at[f, :, x]
            recv = xin_r.at[j, 2 * pair + a]
            pltpu.make_async_copy(src.at[0, 0, :, :, lanes(me, j)], to, recv).start()
            for k in range(1, 8):
                other, device = member(k)
                remote(src.at[0, 0, :, :, lanes(other, j)], to, xin_s.at[j, 2 * pair + a], recv, device).start()

    def leave(j, a, out):
        to = out.at[0, 0, :, :, lanes(me, j)]
        pltpu.make_async_copy(ost.at[j, a, f, :, x], to, out_r.at[a]).start()
        for k in range(1, 8):
            other, device = member(k)
            remote(ost.at[j, a, other % 2, :, other // 2], to, out_s.at[j, a], out_r.at[a], device).start()

    def blank(n):
        dqr[:, n] = jnp.zeros_like(dqr[:, n])
        prc[:, n, :, 0:1, :] = jnp.full_like(prc[:, n, :, 0:1, :], NONE)
        prc[:, n, :, 1:8, :] = jnp.zeros_like(prc[:, n, :, 1:8, :])

    def enter_both(j, carry):
        pl.when(j < nh)(lambda: enter(j, 0))
        pl.when(j >= 1)(lambda: enter(j - 1, 1))
        return carry

    enter(0, 0)
    lax.fori_loop(1, nh + 1, enter_both, 0)

    near.wait()
    for n, dr in enumerate((1, 0, -1)):
        row = h + dr
        inside = jnp.logical_and(row >= 0, row < NROWS)
        for kt in range(4):
            wanted = jnp.where(inside, (kt // 2 * NROWS + row) * 2 + kt % 2, -2)
            for c in range(2):
                found = jnp.where(nb_ref[0, 0, c : c + 1, :] == wanted, 0.0, NONE)
                found = jnp.max(found, axis=-1, keepdims=True)
                tab[n, f, kt : kt + 1, c * TILE : (c + 1) * TILE] = jnp.broadcast_to(found, (1, TILE))
        tab[n, f, 4:8, :] = jnp.zeros((4, 2 * TILE), jnp.float32)
    swap = remote(tab.at[:, f], tab.at[:, f], tab_s, tab_r, (1 - f, h, x))
    swap.start()
    swap.wait()
    bias[1] = tab[1]
    lend = [remote(tab.at[2 * n], bias.at[2 * n], bias_s.at[n], bias_r.at[n], beside[1 - n]) for n in range(2)]
    each(lambda n: lend[1 - n].start())

    @pl.when(h == 0)
    def _():
        blank(0)

    @pl.when(h == NROWS - 1)
    def _():
        blank(1)

    def lend_queries(j):
        for a in range(2):
            await_bytes(qg.at[1, j, a], xin_r.at[j, a])
            each(lambda n: remote(qg.at[1, j, a], qg.at[2 - 2 * n, j, a], halo_s.at[n, j], halo_r.at[1 - n, j], beside[n]).start())

    def return_queries(j):
        each(lambda n: remote(dqs.at[j, 2 * n], dqr.at[j, 1 - n], dq_s.at[n, j], dq_r.at[1 - n, j], beside[n]).start())

    def finish_queries(j):
        each(lambda n: await_bytes(dqr.at[j, n], dq_r.at[n, j]))
        total = dqf[j] + dqr[j, 0].astype(jnp.float32) + dqr[j, 1].astype(jnp.float32)
        ost[j, 0] = total.astype(jnp.bfloat16).reshape(ost.shape[2:])
        leave(j, 0, oq_ref)

    def neighbours_of(action):
        def body(n, carry):
            ahead = jnp.where(n == 0, h - 1, h + 1)
            pl.when(jnp.logical_and(ahead >= 0, ahead < NROWS))(lambda: action(n, (f, ahead, x)))
            return carry

        lax.fori_loop(0, 2, body, 0)

    def weights_beside(j):
        def one(n, device):
            await_bytes(qg.at[2 * n, j], halo_r.at[n, j])
            phase_a(2 * n, j, lax.rem(j, 3), qg, kv, bias, es, dps, ms, pst)
            remote(pst.at[j, 2 * n], prc.at[j, 1 - n], part_s.at[n, j], part_r.at[1 - n, j], device).start()

        neighbours_of(one)

    def gradients(j):
        dka[...] = jnp.zeros_like(dka)
        dva[...] = jnp.zeros_like(dva)

        def one(n, device):
            await_bytes(fin.at[j, 2 * n], fin_r.at[n, j])
            phase_b(2 * n, j, lax.rem(j, 3), qg, kv, es, dps, ms, fin, dka, dva, dqs, dqf)

        neighbours_of(one)
        pl.when(j == nh - 1)(lambda: return_queries(j))
        phase_b(1, j, lax.rem(j, 3), qg, kv, es, dps, ms, fin, dka, dva, dqs, dqf)
        ost[j, 1] = (dka[...] * HD**-0.5).astype(jnp.bfloat16).reshape(ost.shape[2:])
        ost[j, 2] = dva[...].astype(jnp.bfloat16).reshape(ost.shape[2:])
        leave(j, 1, ok_ref)
        leave(j, 2, ov_ref)

    def step(t, carry):
        @pl.when(t + 1 < nh)
        def _():
            lend_queries(t + 1)

        pl.when(t == nh - 2)(lambda: return_queries(0))

        @pl.when(t < nh)
        def _():
            @pl.when(t == 0)
            def _():
                each(lambda n: lend[n].wait_recv())

            for a in range(2):
                await_bytes(kv.at[t, a], xin_r.at[t, 2 + a])
            phase_a(1, t, lax.rem(t, 3), qg, kv, bias, es, dps, ms, pst)
            weights_beside(t)

        @pl.when(jnp.logical_and(t >= 1, t < nh + 1))
        def _():
            j = t - 1
            each(lambda n: await_bytes(prc.at[j, n], part_r.at[n, j]))
            combine(j, pst, prc, fin)
            each(lambda n: remote(fin.at[j, 1], fin.at[j, 2 - 2 * n], fin_s.at[n, j], fin_r.at[1 - n, j], beside[n]).start())

        pl.when(t >= nh - 1)(lambda: return_queries(t - nh + 2))

        @pl.when(t >= 2)
        def _():
            gradients(t - 2)

        pl.when(t == nh)(lambda: finish_queries(0))
        return carry

    lend_queries(0)
    lax.fori_loop(0, nh + 2, step, 0)
    lax.fori_loop(1, nh, lambda j, c: (finish_queries(j), c)[1], 0)

    for a, out in enumerate((oq_ref, ok_ref, ov_ref)):
        await_bytes(out, out_r.at[a])
    each(lambda n: lend[1 - n].wait_send())

    def settle(j, carry):
        sent = dqs.at[j, 0, pl.ds(0, 7 * TILE // 2)]
        for a in range(4):
            await_bytes(sent, xin_s.at[j, a])
        for a in range(3):
            await_bytes(sent, out_s.at[j, a])

        def lent(n):
            await_bytes(qg.at[1, j], halo_s.at[n, j])
            await_bytes(prc.at[j, n], part_s.at[n, j])
            await_bytes(prc.at[j, n], fin_s.at[n, j])
            await_bytes(dqr.at[j, n], dq_s.at[n, j])

        each(lent)
        return carry

    lax.fori_loop(0, nh, settle, 0)


def hand_over(aq, ak, av, bq, bk, bv, room, into, out):
    pieces = [(n, c, a.at[0, 0, c], b.at[0, 0, c]) for n, (a, b) in enumerate(((aq, bq), (ak, bk), (av, bv))) for c in range(2)]
    ins = [pltpu.make_async_copy(a, room.at[n, c], into.at[n, c]) for n, c, a, b in pieces]
    outs = [pltpu.make_async_copy(room.at[n, c], b, out.at[n, c]) for n, c, a, b in pieces]
    for copy in ins:
        copy.start()
    for arrived, copy in zip(ins, outs):
        arrived.wait()
        copy.start()
    for copy in outs:
        copy.wait()


def local(queries, keys, values, out_grad, neighbours):
    nh = queries.shape[-1] // HD // 8
    tiles = (2, 2, 4, TILE // 4, HD)
    bf, f32 = jnp.bfloat16, jnp.float32
    dma = pltpu.SemaphoreType.DMA
    any_spec = pl.BlockSpec(memory_space=pl.ANY)
    shape = jax.ShapeDtypeStruct(queries.shape, bf)
    products = 5 * 512 * 1536 * HD * nh
    grads = pl.pallas_call(
        functools.partial(kernel, nh),
        out_shape=(shape, shape, shape),
        in_specs=[any_spec] * 5,
        out_specs=[any_spec] * 3,
        scratch_shapes=[
            pltpu.VMEM(neighbours.shape, jnp.int32),
            pltpu.VMEM((3, nh, 2) + tiles, bf),
            pltpu.VMEM((nh, 2) + tiles, bf),
            pltpu.VMEM((3, 2, 8, 256), f32),
            pltpu.VMEM((3, 2, 8, 256), f32),
            pltpu.VMEM((3, 6, 4, TILE, 256), f32),
            pltpu.VMEM((3, 6, 4, TILE, 256), f32),
            pltpu.VMEM((3, 6, 8, 256), f32),
            pltpu.VMEM((nh, 3, 2, 8, 256), f32),
            pltpu.VMEM((nh, 2, 2, 8, 256), f32),
            pltpu.VMEM((nh, 3, 2, 8, 256), f32),
            pltpu.VMEM((4, TILE, HD), f32),
            pltpu.VMEM((4, TILE, HD), f32),
            pltpu.VMEM((nh, 3, 512, HD), bf),
            pltpu.VMEM((nh, 2, 512, HD), bf),
            pltpu.VMEM((nh, 512, HD), f32),
            pltpu.VMEM((nh, 3) + tiles, bf),
            dma((nh, 4)), dma((nh, 4)),
            dma((2, nh)), dma((2, nh)),
            dma((2, nh)), dma((2, nh)),
            dma((2, nh)), dma((2, nh)),
            dma((2, nh)), dma((2, nh)),
            dma((nh, 3)), dma((3,)),
            dma(()), dma(()),
            dma((2,)), dma((2,)),
            dma(()),
        ],
        compiler_params=pltpu.CompilerParams(
            collective_id=0, has_side_effects=True, vmem_limit_bytes=60 * 1024 * 1024
        ),
        cost_estimate=pl.CostEstimate(
            flops=2 * products, bytes_accessed=7 * 2 * queries.size, transcendentals=512 * 1536 * nh
        ),
        name="window_backward",
    )(queries, keys, values, out_grad, neighbours)
    return pl.pallas_call(
        hand_over,
        out_shape=(shape, shape, shape),
        in_specs=[any_spec] * 3,
        out_specs=[any_spec] * 3,
        scratch_shapes=[pltpu.VMEM((3,) + queries.shape[2:], bf), dma((3, 2)), dma((3, 2))],
        compiler_params=pltpu.CompilerParams(vmem_limit_bytes=60 * 1024 * 1024),
        name="hand_over",
    )(*grads)


def solution(mesh):
    whole = P("frames", "rows", None, "heads", None)
    return jax.shard_map(
        local,
        mesh=mesh,
        in_specs=(whole, whole, whole, whole, P("frames", "rows", None, None)),
        out_specs=(whole, whole, whole),
        check_vma=False,
    )
```

```python
import functools

import jax
import jax.numpy as jnp
from jax import lax
from jax.experimental import pallas as pl
from jax.experimental.pallas import tpu as pltpu
from jax.sharding import PartitionSpec as P

MESH = pl.DeviceIdType.MESH
HD = 128
TILE = 128
NROWS = 16
LOG2E = 1.4426950408889634
NONE = -1e30
NT = (((1,), (1,)), ((), ()))
NN = (((1,), (0,)), ((), ()))
TN = (((0,), (0,)), ((), ()))


def dot(a, b, dims):
    return lax.dot_general(a, b, dims, preferred_element_type=jnp.float32)


def phase_a(s, j, p, qg, kv, bias, es, dps, ms, pst):
    scale = LOG2E * HD**-0.5

    def block(f, carry):
        i = 2 * s + f
        q = qg[s, j, 0, f].reshape(2 * TILE, HD)
        g = qg[s, j, 1, f].reshape(2 * TILE, HD)
        peaks, sums, prods = [], [], []
        for kt in range(4):
            k = kv[j, 0, kt // 2, kt % 2].reshape(TILE, HD)
            v = kv[j, 1, kt // 2, kt % 2].reshape(TILE, HD)
            st = dot(k, q, NT) * scale
            m = jnp.max(st, axis=0, keepdims=True)
            e = jnp.exp2(st - m)
            dp = dot(v, g, NT)
            es[p, i, kt] = e
            dps[p, i, kt] = dp
            mb = m + bias[s, f, kt : kt + 1, :]
            ms[p, i, kt : kt + 1, :] = mb
            peaks.append(mb)
            sums.append(jnp.sum(e, axis=0, keepdims=True))
            prods.append(jnp.sum(e * dp, axis=0, keepdims=True))
        top = functools.reduce(jnp.maximum, peaks)
        ws = [jnp.exp2(mb - top) for mb in peaks]
        pst[j, s, f, 0:1, :] = top
        pst[j, s, f, 1:2, :] = sum(w * l for w, l in zip(ws, sums))
        pst[j, s, f, 2:3, :] = sum(w * d for w, d in zip(ws, prods))
        return carry

    block(0, 0)
    block(1, 0)


def combine(j, pst, prc, fin):
    for f in range(2):
        parts = [pst[j, 1, f], prc[j, 0, f], prc[j, 1, f]]
        top = functools.reduce(jnp.maximum, [x[0:1] for x in parts])
        ws = [jnp.exp2(x[0:1] - top) for x in parts]
        total = sum(w * x[1:2] for w, x in zip(ws, parts))
        prod = sum(w * x[2:3] for w, x in zip(ws, parts))
        fin[j, 1, f, 0:1, :] = top + jnp.log2(total)
        fin[j, 1, f, 1:2, :] = prod / total


def phase_b(s, j, p, qg, kv, es, dps, ms, fin, dka, dva, dqs, dqf):
    scale = HD**-0.5

    def block(f, carry):
        i = 2 * s + f
        q = qg[s, j, 0, f].reshape(2 * TILE, HD)
        g = qg[s, j, 1, f].reshape(2 * TILE, HD)
        lse = fin[j, s, f, 0:1, :]
        delta = fin[j, s, f, 1:2, :]
        probs, grads = [], []
        for kt in range(4):
            r = jnp.exp2(ms[p, i, kt : kt + 1, :] - lse)
            prob = es[p, i, kt] * r
            ds = (prob * (dps[p, i, kt] - delta)).astype(jnp.bfloat16)
            probs.append(prob.astype(jnp.bfloat16))
            grads.append(ds)
        probs, grads = jnp.concatenate(probs), jnp.concatenate(grads)
        dva[...] += dot(probs, g, NN).reshape(dva.shape)
        dka[...] += dot(grads, q, NN).reshape(dka.shape)
        dq = dot(kv[j, 0].reshape(4 * TILE, HD), grads, TN).T * scale
        rows = pl.ds(pl.multiple_of(f * 2 * TILE, 2 * TILE), 2 * TILE)
        if isinstance(s, int):
            dqf[j, rows] = dq
        else:
            dqs[j, s, rows] = dq.astype(jnp.bfloat16)
        return carry

    block(0, 0)
    block(1, 0)


def kernel(nh, q_ref, k_ref, v_ref, g_ref, nb_hbm, oq_ref, ok_ref, ov_ref,
           nb_ref, qg, kv, tab, bias, es, dps, ms, pst, prc, fin, dka, dva, dqs, dqr, dqf, ost,
           xin_s, xin_r, halo_s, halo_r, part_s, part_r, fin_s, fin_r, dq_s, dq_r, out_s, out_r,
           tab_s, tab_r, bias_s, bias_r, nb_s, dqh_s, dqh_r):
    f = lax.axis_index("frames")
    h = lax.axis_index("rows")
    x = lax.axis_index("heads")
    me = x * 2 + f
    beside = (f, jnp.maximum(h - 1, 0), x), (f, jnp.minimum(h + 1, NROWS - 1), x)
    held = h > 0, h < NROWS - 1

    def member(k):
        other = lax.rem(me + k, 8)
        return other, (other % 2, h, other // 2)

    near = pltpu.make_async_copy(nb_hbm, nb_ref, nb_s)
    near.start()
    barrier = pltpu.get_barrier_semaphore()
    for k in range(1, 8):
        pl.semaphore_signal(barrier, inc=1, device_id=member(k)[1], device_id_type=MESH)
    for n in range(2):

        @pl.when(held[n])
        def _():
            pl.semaphore_signal(barrier, inc=1, device_id=beside[n], device_id_type=MESH)

    near.wait()
    for n, dr in enumerate((1, 0, -1)):
        row = h + dr
        inside = jnp.logical_and(row >= 0, row < NROWS)
        for kt in range(4):
            wanted = jnp.where(inside, (kt // 2 * NROWS + row) * 2 + kt % 2, -2)
            for c in range(2):
                found = jnp.where(nb_ref[0, 0, c : c + 1, :] == wanted, 0.0, NONE)
                found = jnp.max(found, axis=-1, keepdims=True)
                tab[n, f, kt : kt + 1, c * TILE : (c + 1) * TILE] = jnp.broadcast_to(found, (1, TILE))
        tab[n, f, 4:8, :] = jnp.zeros((4, 2 * TILE), jnp.float32)

    pl.semaphore_wait(barrier, 7 + held[0].astype(jnp.int32) + held[1].astype(jnp.int32))

    def remote(src, dst, send, recv, device):
        return pltpu.make_async_remote_copy(
            src_ref=src, dst_ref=dst, send_sem=send, recv_sem=recv, device_id=device, device_id_type=MESH
        )

    def await_bytes(ref, sem):
        pltpu.make_async_copy(ref, ref, sem).wait()

    def each(action):
        for n in range(2):
            pl.when(held[n])(functools.partial(action, n))

    def lanes(owner, j):
        return pl.ds(pl.multiple_of((owner * nh + j) * HD, HD), HD)

    def enter(j, pair):
        sides = ((q_ref, qg.at[1, j, 0]), (g_ref, qg.at[1, j, 1])), ((k_ref, kv.at[j, 0]), (v_ref, kv.at[j, 1]))
        for a, (src, dst) in enumerate(sides[pair]):
            to = dst.at[f, :, x]
            recv = xin_r.at[j, 2 * pair + a]
            pltpu.make_async_copy(src.at[0, 0, :, :, lanes(me, j)], to, recv).start()
            for k in range(1, 8):
                other, device = member(k)
                remote(src.at[0, 0, :, :, lanes(other, j)], to, xin_s.at[j, 2 * pair + a], recv, device).start()

    def leave(j, a, out):
        to = out.at[0, 0, :, :, lanes(me, j)]
        pltpu.make_async_copy(ost.at[j, a, f, :, x], to, out_r.at[a]).start()
        for k in range(1, 8):
            other, device = member(k)
            remote(ost.at[j, a, other % 2, :, other // 2], to, out_s.at[j, a], out_r.at[a], device).start()

    def blank(n):
        dqr[:, n] = jnp.zeros_like(dqr[:, n])
        prc[:, n, :, 0:1, :] = jnp.full_like(prc[:, n, :, 0:1, :], NONE)
        prc[:, n, :, 1:8, :] = jnp.zeros_like(prc[:, n, :, 1:8, :])

    def enter_both(j, carry):
        pl.when(j < nh)(lambda: enter(j, 0))
        pl.when(j >= 1)(lambda: enter(j - 1, 1))
        return carry

    enter(0, 0)
    swap = remote(tab.at[:, f], tab.at[:, f], tab_s, tab_r, (1 - f, h, x))
    swap.start()
    lax.fori_loop(1, nh + 1, enter_both, 0)

    def lend_queries(j):
        for a in range(2):
            await_bytes(qg.at[1, j, a], xin_r.at[j, a])
            each(lambda n: remote(qg.at[1, j, a], qg.at[2 - 2 * n, j, a], halo_s.at[n, j], halo_r.at[1 - n, j], beside[n]).start())

    def return_queries(j):
        each(lambda n: remote(dqs.at[j, 2 * n], dqr.at[j, 1 - n], dq_s.at[n, j], dq_r.at[1 - n, j], beside[n]).start())

    def return_half(half):
        rows = pl.ds(half * 2 * TILE, 2 * TILE)
        each(lambda n: remote(dqs.at[nh - 1, 2 * n, rows], dqr.at[nh - 1, 1 - n, rows], dqh_s.at[n, half], dqh_r.at[1 - n, half], beside[n]).start())

    def finish_half(half):
        j, rows = nh - 1, pl.ds(half * 2 * TILE, 2 * TILE)
        each(lambda n: await_bytes(dqr.at[j, n, rows], dqh_r.at[n, half]))
        total = dqf[j, rows] + dqr[j, 0, rows].astype(jnp.float32) + dqr[j, 1, rows].astype(jnp.float32)
        ost[j, 0, half] = total.astype(jnp.bfloat16).reshape(ost.shape[3:])
        to = oq_ref.at[0, 0, :, :, lanes(me, j)]

        def across(k):
            xk = lax.rem(x + k, 4)
            remote(ost.at[j, 0, half, :, xk], to, out_s.at[j, 0], out_r.at[0], (half, h, xk)).start()

        @pl.when(f == half)
        def _():
            pltpu.make_async_copy(ost.at[j, 0, half, :, x], to, out_r.at[0]).start()

        pl.when(f != half)(lambda: across(0))
        for k in range(1, 4):
            across(k)

    def finish_queries(j):
        each(lambda n: await_bytes(dqr.at[j, n], dq_r.at[n, j]))
        total = dqf[j] + dqr[j, 0].astype(jnp.float32) + dqr[j, 1].astype(jnp.float32)
        ost[j, 0] = total.astype(jnp.bfloat16).reshape(ost.shape[2:])
        leave(j, 0, oq_ref)

    def neighbours_of(action):
        def body(n, carry):
            ahead = jnp.where(n == 0, h - 1, h + 1)
            pl.when(jnp.logical_and(ahead >= 0, ahead < NROWS))(lambda: action(n, (f, ahead, x)))
            return carry

        lax.fori_loop(0, 2, body, 0)

    def weights_beside(j):
        def one(n, device):
            await_bytes(qg.at[2 * n, j], halo_r.at[n, j])
            phase_a(2 * n, j, lax.rem(j, 3), qg, kv, bias, es, dps, ms, pst)
            remote(pst.at[j, 2 * n], prc.at[j, 1 - n], part_s.at[n, j], part_r.at[1 - n, j], device).start()

        neighbours_of(one)

    def gradients(j):
        dka[...] = jnp.zeros_like(dka)
        dva[...] = jnp.zeros_like(dva)

        def one(n, device):
            await_bytes(fin.at[j, 2 * n], fin_r.at[n, j])
            phase_b(2 * n, j, lax.rem(j, 3), qg, kv, es, dps, ms, fin, dka, dva, dqs, dqf)

        neighbours_of(one)

        @pl.when(j == nh - 1)
        def _():
            return_half(0)
            return_half(1)

        phase_b(1, j, lax.rem(j, 3), qg, kv, es, dps, ms, fin, dka, dva, dqs, dqf)
        ost[j, 1] = (dka[...] * HD**-0.5).astype(jnp.bfloat16).reshape(ost.shape[2:])
        ost[j, 2] = dva[...].astype(jnp.bfloat16).reshape(ost.shape[2:])
        leave(j, 1, ok_ref)
        leave(j, 2, ov_ref)

    def step(t, carry):
        pl.when(t + 1 < nh)(lambda: lend_queries(t + 1))

        pl.when(t == nh - 1)(lambda: return_queries(0))

        @pl.when(t < nh)
        def _():
            for a in range(2):
                await_bytes(kv.at[t, a], xin_r.at[t, 2 + a])
            phase_a(1, t, lax.rem(t, 3), qg, kv, bias, es, dps, ms, pst)

        pl.when(t >= 2)(lambda: gradients(t - 2))

        @pl.when(jnp.logical_and(t >= 1, t < nh + 1))
        def _():
            j = t - 1
            each(lambda n: await_bytes(prc.at[j, n], part_r.at[n, j]))
            combine(j, pst, prc, fin)
            each(lambda n: remote(fin.at[j, 1], fin.at[j, 2 - 2 * n], fin_s.at[n, j], fin_r.at[1 - n, j], beside[n]).start())

        @pl.when(t < nh)
        def _():
            pl.when(t == 0)(lambda: each(lambda n: lend[n].wait_recv()))
            weights_beside(t)

        @pl.when(t == nh - 1)
        def _():
            return_queries(1)
            finish_queries(0)

        @pl.when(t == nh)
        def _():
            return_queries(2)
            return_queries(3)
            finish_queries(1)

        return carry

    lend_queries(0)
    swap.wait()
    bias[1] = tab[1]
    lend = [remote(tab.at[2 * n], bias.at[2 * n], bias_s.at[n], bias_r.at[n], beside[1 - n]) for n in range(2)]
    each(lambda n: lend[1 - n].start())

    @pl.when(h == 0)
    def _():
        blank(0)

    @pl.when(h == NROWS - 1)
    def _():
        blank(1)

    lax.fori_loop(0, nh + 2, step, 0)
    lax.fori_loop(2, nh - 1, lambda j, c: (finish_queries(j), c)[1], 0)
    finish_half(0)
    finish_half(1)

    for a, out in enumerate((oq_ref, ok_ref, ov_ref)):
        await_bytes(out, out_r.at[a])
    each(lambda n: lend[1 - n].wait_send())

    def settle(j, carry):
        sent = dqs.at[j, 0, pl.ds(0, 7 * TILE // 2)]
        for a in range(4):
            await_bytes(sent, xin_s.at[j, a])
        for a in range(3):
            await_bytes(sent, out_s.at[j, a])

        def lent(n):
            await_bytes(qg.at[1, j], halo_s.at[n, j])
            await_bytes(prc.at[j, n], part_s.at[n, j])
            await_bytes(prc.at[j, n], fin_s.at[n, j])
            pl.when(j < nh - 1)(lambda: await_bytes(dqr.at[j, n], dq_s.at[n, j]))

        each(lent)
        return carry

    lax.fori_loop(0, nh, settle, 0)
    for half in range(2):
        each(lambda n: await_bytes(dqr.at[nh - 1, n, pl.ds(0, 2 * TILE)], dqh_s.at[n, half]))


def hand_over(aq, ak, av, bq, bk, bv, room, into, out):
    pieces = [(n, c, a.at[0, 0, c], b.at[0, 0, c]) for n, (a, b) in enumerate(((aq, bq), (ak, bk), (av, bv))) for c in range(2)]
    ins = [pltpu.make_async_copy(a, room.at[n, c], into.at[n, c]) for n, c, a, b in pieces]
    outs = [pltpu.make_async_copy(room.at[n, c], b, out.at[n, c]) for n, c, a, b in pieces]
    for copy in ins:
        copy.start()
    for arrived, copy in zip(ins, outs):
        arrived.wait()
        copy.start()
    for copy in outs:
        copy.wait()


def local(queries, keys, values, out_grad, neighbours):
    nh = queries.shape[-1] // HD // 8
    tiles = (2, 2, 4, TILE // 4, HD)
    bf, f32 = jnp.bfloat16, jnp.float32
    dma = pltpu.SemaphoreType.DMA
    any_spec = pl.BlockSpec(memory_space=pl.ANY)
    shape = jax.ShapeDtypeStruct(queries.shape, bf)
    products = 5 * 512 * 1536 * HD * nh
    grads = pl.pallas_call(
        functools.partial(kernel, nh),
        out_shape=(shape, shape, shape),
        in_specs=[any_spec] * 5,
        out_specs=[any_spec] * 3,
        scratch_shapes=[
            pltpu.VMEM(neighbours.shape, jnp.int32),
            pltpu.VMEM((3, nh, 2) + tiles, bf),
            pltpu.VMEM((nh, 2) + tiles, bf),
            pltpu.VMEM((3, 2, 8, 256), f32),
            pltpu.VMEM((3, 2, 8, 256), f32),
            pltpu.VMEM((3, 6, 4, TILE, 256), f32),
            pltpu.VMEM((3, 6, 4, TILE, 256), f32),
            pltpu.VMEM((3, 6, 8, 256), f32),
            pltpu.VMEM((nh, 3, 2, 8, 256), f32),
            pltpu.VMEM((nh, 2, 2, 8, 256), f32),
            pltpu.VMEM((nh, 3, 2, 8, 256), f32),
            pltpu.VMEM((4, TILE, HD), f32),
            pltpu.VMEM((4, TILE, HD), f32),
            pltpu.VMEM((nh, 3, 512, HD), bf),
            pltpu.VMEM((nh, 2, 512, HD), bf),
            pltpu.VMEM((nh, 512, HD), f32),
            pltpu.VMEM((nh, 3) + tiles, bf),
            dma((nh, 4)), dma((nh, 4)),
            dma((2, nh)), dma((2, nh)),
            dma((2, nh)), dma((2, nh)),
            dma((2, nh)), dma((2, nh)),
            dma((2, nh)), dma((2, nh)),
            dma((nh, 3)), dma((3,)),
            dma(()), dma(()),
            dma((2,)), dma((2,)),
            dma(()),
            dma((2, 2)), dma((2, 2)),
        ],
        compiler_params=pltpu.CompilerParams(
            collective_id=0, has_side_effects=True, vmem_limit_bytes=60 * 1024 * 1024
        ),
        cost_estimate=pl.CostEstimate(
            flops=2 * products, bytes_accessed=7 * 2 * queries.size, transcendentals=512 * 1536 * nh
        ),
        name="window_backward",
    )(queries, keys, values, out_grad, neighbours)
    return pl.pallas_call(
        hand_over,
        out_shape=(shape, shape, shape),
        in_specs=[any_spec] * 3,
        out_specs=[any_spec] * 3,
        scratch_shapes=[pltpu.VMEM((3,) + queries.shape[2:], bf), dma((3, 2)), dma((3, 2))],
        compiler_params=pltpu.CompilerParams(vmem_limit_bytes=60 * 1024 * 1024),
        name="hand_over",
    )(*grads)


def solution(mesh):
    whole = P("frames", "rows", None, "heads", None)
    return jax.shard_map(
        local,
        mesh=mesh,
        in_specs=(whole, whole, whole, whole, P("frames", "rows", None, None)),
        out_specs=(whole, whole, whole),
        check_vma=False,
    )
```

```python
import functools

import jax
import jax.numpy as jnp
from jax import lax
from jax.experimental import pallas as pl
from jax.experimental.pallas import tpu as pltpu
from jax.sharding import PartitionSpec as P

MESH = pl.DeviceIdType.MESH
HD = 128
TILE = 128
NROWS = 16
LOG2E = 1.4426950408889634
NONE = -1e30
NT = (((1,), (1,)), ((), ()))
NN = (((1,), (0,)), ((), ()))
TN = (((0,), (0,)), ((), ()))


def dot(a, b, dims):
    return lax.dot_general(a, b, dims, preferred_element_type=jnp.float32)


def phase_a(s, j, p, qg, kv, bias, es, dps, ms, pst):
    scale = LOG2E * HD**-0.5

    def block(f, carry):
        i = 2 * s + f
        q = qg[s, j, 0, f].reshape(2 * TILE, HD)
        g = qg[s, j, 1, f].reshape(2 * TILE, HD)
        peaks, sums, prods = [], [], []
        for kt in range(4):
            k = kv[j, 0, kt // 2, kt % 2].reshape(TILE, HD)
            v = kv[j, 1, kt // 2, kt % 2].reshape(TILE, HD)
            st = dot(k, q, NT) * scale
            m = jnp.max(st, axis=0, keepdims=True)
            e = jnp.exp2(st - m)
            dp = dot(v, g, NT)
            es[p, i, kt] = e
            dps[p, i, kt] = dp
            mb = m + bias[s, f, kt : kt + 1, :]
            ms[p, i, kt : kt + 1, :] = mb
            peaks.append(mb)
            sums.append(jnp.sum(e, axis=0, keepdims=True))
            prods.append(jnp.sum(e * dp, axis=0, keepdims=True))
        top = functools.reduce(jnp.maximum, peaks)
        ws = [jnp.exp2(mb - top) for mb in peaks]
        pst[j, s, 3 * f : 3 * f + 1, :] = top
        pst[j, s, 3 * f + 1 : 3 * f + 2, :] = sum(w * l for w, l in zip(ws, sums))
        pst[j, s, 3 * f + 2 : 3 * f + 3, :] = sum(w * d for w, d in zip(ws, prods))
        return carry

    block(0, 0)
    block(1, 0)


def combine(j, pst, prc, fin):
    for f in range(2):
        rows = slice(3 * f, 3 * f + 3)
        parts = [pst[j, 1, rows], prc[j, 0, rows], prc[j, 1, rows]]
        top = functools.reduce(jnp.maximum, [x[0:1] for x in parts])
        ws = [jnp.exp2(x[0:1] - top) for x in parts]
        total = sum(w * x[1:2] for w, x in zip(ws, parts))
        prod = sum(w * x[2:3] for w, x in zip(ws, parts))
        fin[j, 1, 2 * f : 2 * f + 1, :] = top + jnp.log2(total)
        fin[j, 1, 2 * f + 1 : 2 * f + 2, :] = prod / total


def phase_b(s, j, p, qg, kv, es, dps, ms, fin, dka, dva, dqs, dqf):
    scale = HD**-0.5

    def block(f, carry):
        i = 2 * s + f
        q = qg[s, j, 0, f].reshape(2 * TILE, HD)
        g = qg[s, j, 1, f].reshape(2 * TILE, HD)
        lse = fin[j, s, 2 * f : 2 * f + 1, :]
        delta = fin[j, s, 2 * f + 1 : 2 * f + 2, :]
        probs, grads = [], []
        for kt in range(4):
            r = jnp.exp2(ms[p, i, kt : kt + 1, :] - lse)
            prob = es[p, i, kt] * r
            ds = (prob * (dps[p, i, kt] - delta)).astype(jnp.bfloat16)
            probs.append(prob.astype(jnp.bfloat16))
            grads.append(ds)
        probs, grads = jnp.concatenate(probs), jnp.concatenate(grads)
        dva[...] += dot(probs, g, NN).reshape(dva.shape)
        dka[...] += dot(grads, q, NN).reshape(dka.shape)
        dq = dot(kv[j, 0].reshape(4 * TILE, HD), grads, TN).T * scale
        rows = pl.ds(pl.multiple_of(f * 2 * TILE, 2 * TILE), 2 * TILE)
        if isinstance(s, int):
            dqf[j, rows] = dq
        else:
            dqs[j, s, rows] = dq.astype(jnp.bfloat16)
        return carry

    block(0, 0)
    block(1, 0)


def kernel(nh, q_ref, k_ref, v_ref, g_ref, nb_hbm, oq_ref, ok_ref, ov_ref,
           nb_ref, qg, kv, tab, bias, es, dps, ms, pst, prc, fin, dka, dva, dqs, dqr, dqf, ost,
           xin_s, xin_r, halo_s, halo_r, part_s, part_r, fin_s, fin_r, dq_s, dq_r, out_s, out_r,
           tab_s, tab_r, bias_s, bias_r, nb_s, dqh_s, dqh_r):
    f = lax.axis_index("frames")
    h = lax.axis_index("rows")
    x = lax.axis_index("heads")
    me = x * 2 + f
    beside = (f, jnp.maximum(h - 1, 0), x), (f, jnp.minimum(h + 1, NROWS - 1), x)
    held = h > 0, h < NROWS - 1

    def member(k):
        other = lax.rem(me + k, 8)
        return other, (other % 2, h, other // 2)

    near = pltpu.make_async_copy(nb_hbm, nb_ref, nb_s)
    near.start()
    barrier = pltpu.get_barrier_semaphore()
    for k in range(1, 8):
        pl.semaphore_signal(barrier, inc=1, device_id=member(k)[1], device_id_type=MESH)
    for n in range(2):

        @pl.when(held[n])
        def _():
            pl.semaphore_signal(barrier, inc=1, device_id=beside[n], device_id_type=MESH)

    pl.semaphore_wait(barrier, 7 + held[0].astype(jnp.int32) + held[1].astype(jnp.int32))

    def remote(src, dst, send, recv, device):
        return pltpu.make_async_remote_copy(
            src_ref=src, dst_ref=dst, send_sem=send, recv_sem=recv, device_id=device, device_id_type=MESH
        )

    def await_bytes(ref, sem):
        pltpu.make_async_copy(ref, ref, sem).wait()

    def each(action):
        for n in range(2):
            pl.when(held[n])(functools.partial(action, n))

    def lanes(owner, j):
        return pl.ds(pl.multiple_of((owner * nh + j) * HD, HD), HD)

    def enter(j, pair):
        sides = ((q_ref, qg.at[1, j, 0]), (g_ref, qg.at[1, j, 1])), ((k_ref, kv.at[j, 0]), (v_ref, kv.at[j, 1]))
        for a, (src, dst) in enumerate(sides[pair]):
            to = dst.at[f, :, x]
            recv = xin_r.at[j, 2 * pair + a]
            pltpu.make_async_copy(src.at[0, 0, :, :, lanes(me, j)], to, recv).start()
            for k in range(1, 8):
                other, device = member(k)
                remote(src.at[0, 0, :, :, lanes(other, j)], to, xin_s.at[j, 2 * pair + a], recv, device).start()

    def leave(j, a, out):
        to = out.at[0, 0, :, :, lanes(me, j)]
        pltpu.make_async_copy(ost.at[j, a, f, :, x], to, out_r.at[a]).start()
        for k in range(1, 8):
            other, device = member(k)
            remote(ost.at[j, a, other % 2, :, other // 2], to, out_s.at[j, a], out_r.at[a], device).start()

    def blank(n):
        dqr[:, n] = jnp.zeros_like(dqr[:, n])
        prc[:, n] = jnp.full_like(prc[:, n], NONE)

    def enter_both(j, carry):
        pl.when(j < nh)(lambda: enter(j, 0))
        pl.when(j >= 1)(lambda: enter(j - 1, 1))
        return carry

    enter(0, 0)
    lax.fori_loop(1, nh + 1, enter_both, 0)

    def lend_queries(j):
        for a in range(2):
            await_bytes(qg.at[1, j, a], xin_r.at[j, a])
            each(lambda n: remote(qg.at[1, j, a], qg.at[2 - 2 * n, j, a], halo_s.at[n, j], halo_r.at[1 - n, j], beside[n]).start())

    def return_queries(j):
        each(lambda n: remote(dqs.at[j, 2 * n], dqr.at[j, 1 - n], dq_s.at[n, j], dq_r.at[1 - n, j], beside[n]).start())

    def return_half(half):
        rows = pl.ds(half * 2 * TILE, 2 * TILE)
        each(lambda n: remote(dqs.at[nh - 1, 2 * n, rows], dqr.at[nh - 1, 1 - n, rows], dqh_s.at[n, half], dqh_r.at[1 - n, half], beside[n]).start())

    def finish_half(half):
        j, rows = nh - 1, pl.ds(half * 2 * TILE, 2 * TILE)
        each(lambda n: await_bytes(dqr.at[j, n, rows], dqh_r.at[n, half]))
        total = dqf[j, rows] + dqr[j, 0, rows].astype(jnp.float32) + dqr[j, 1, rows].astype(jnp.float32)
        ost[j, 0, half] = total.astype(jnp.bfloat16).reshape(ost.shape[3:])
        to = oq_ref.at[0, 0, :, :, lanes(me, j)]

        def across(k):
            xk = lax.rem(x + k, 4)
            remote(ost.at[j, 0, half, :, xk], to, out_s.at[j, 0], out_r.at[0], (half, h, xk)).start()

        @pl.when(f == half)
        def _():
            pltpu.make_async_copy(ost.at[j, 0, half, :, x], to, out_r.at[0]).start()

        pl.when(f != half)(lambda: across(0))
        for k in range(1, 4):
            across(k)

    def finish_queries(j):
        each(lambda n: await_bytes(dqr.at[j, n], dq_r.at[n, j]))
        total = dqf[j] + dqr[j, 0].astype(jnp.float32) + dqr[j, 1].astype(jnp.float32)
        ost[j, 0] = total.astype(jnp.bfloat16).reshape(ost.shape[2:])
        leave(j, 0, oq_ref)

    def neighbours_of(action):
        def body(n, carry):
            ahead = jnp.where(n == 0, h - 1, h + 1)
            pl.when(jnp.logical_and(ahead >= 0, ahead < NROWS))(lambda: action(n, (f, ahead, x)))
            return carry

        lax.fori_loop(0, 2, body, 0)

    def weights_beside(j):
        def one(n, device):
            await_bytes(qg.at[2 * n, j], halo_r.at[n, j])
            phase_a(2 * n, j, lax.rem(j, 3), qg, kv, bias, es, dps, ms, pst)
            remote(pst.at[j, 2 * n], prc.at[j, 1 - n], part_s.at[n, j], part_r.at[1 - n, j], device).start()

        neighbours_of(one)

    def gradients(j):
        dka[...] = jnp.zeros_like(dka)
        dva[...] = jnp.zeros_like(dva)

        def one(n, device):
            await_bytes(fin.at[j, 2 * n], fin_r.at[n, j])
            phase_b(2 * n, j, lax.rem(j, 3), qg, kv, es, dps, ms, fin, dka, dva, dqs, dqf)

        neighbours_of(one)

        @pl.when(j == nh - 1)
        def _():
            return_half(0)
            return_half(1)

        phase_b(1, j, lax.rem(j, 3), qg, kv, es, dps, ms, fin, dka, dva, dqs, dqf)
        ost[j, 1] = (dka[...] * HD**-0.5).astype(jnp.bfloat16).reshape(ost.shape[2:])
        ost[j, 2] = dva[...].astype(jnp.bfloat16).reshape(ost.shape[2:])
        leave(j, 1, ok_ref)
        leave(j, 2, ov_ref)

    def step(t, carry):
        pl.when(t + 1 < nh)(lambda: lend_queries(t + 1))

        pl.when(t == nh - 1)(lambda: return_queries(0))

        @pl.when(t < nh)
        def _():
            for a in range(2):
                await_bytes(kv.at[t, a], xin_r.at[t, 2 + a])
            phase_a(1, t, lax.rem(t, 3), qg, kv, bias, es, dps, ms, pst)

        pl.when(t >= 2)(lambda: gradients(t - 2))

        @pl.when(jnp.logical_and(t >= 1, t < nh + 1))
        def _():
            j = t - 1
            each(lambda n: await_bytes(prc.at[j, n], part_r.at[n, j]))
            combine(j, pst, prc, fin)
            each(lambda n: remote(fin.at[j, 1], fin.at[j, 2 - 2 * n], fin_s.at[n, j], fin_r.at[1 - n, j], beside[n]).start())

        @pl.when(t < nh)
        def _():
            pl.when(t == 0)(lambda: each(lambda n: lend[n].wait_recv()))
            weights_beside(t)

        @pl.when(t == nh - 1)
        def _():
            return_queries(1)
            finish_queries(0)

        @pl.when(t == nh)
        def _():
            return_queries(2)
            return_queries(3)
            finish_queries(1)

        return carry

    near.wait()
    for n, dr in enumerate((1, 0, -1)):
        row = h + dr
        inside = jnp.logical_and(row >= 0, row < NROWS)
        for kt in range(4):
            wanted = jnp.where(inside, (kt // 2 * NROWS + row) * 2 + kt % 2, -2)
            for c in range(2):
                found = jnp.where(nb_ref[0, 0, c : c + 1, :] == wanted, 0.0, NONE)
                found = jnp.max(found, axis=-1, keepdims=True)
                tab[n, f, kt : kt + 1, c * TILE : (c + 1) * TILE] = jnp.broadcast_to(found, (1, TILE))
        tab[n, f, 4:8, :] = jnp.zeros((4, 2 * TILE), jnp.float32)
    swap = remote(tab.at[:, f], tab.at[:, f], tab_s, tab_r, (1 - f, h, x))
    swap.start()

    lend_queries(0)
    swap.wait()
    bias[1] = tab[1]
    lend = [remote(tab.at[2 * n], bias.at[2 * n], bias_s.at[n], bias_r.at[n], beside[1 - n]) for n in range(2)]
    each(lambda n: lend[1 - n].start())

    @pl.when(h == 0)
    def _():
        blank(0)

    @pl.when(h == NROWS - 1)
    def _():
        blank(1)

    lax.fori_loop(0, nh + 2, step, 0)
    lax.fori_loop(2, nh - 1, lambda j, c: (finish_queries(j), c)[1], 0)
    finish_half(0)
    finish_half(1)

    each(lambda n: lend[1 - n].wait_send())

    def settle(j, carry):
        sent = dqs.at[j, 0, pl.ds(0, 7 * TILE // 2)]
        for a in range(4):
            await_bytes(sent, xin_s.at[j, a])
        for a in range(3):
            await_bytes(sent, out_s.at[j, a])

        def lent(n):
            await_bytes(qg.at[1, j], halo_s.at[n, j])
            await_bytes(prc.at[j, n], part_s.at[n, j])
            await_bytes(prc.at[j, n], fin_s.at[n, j])
            pl.when(j < nh - 1)(lambda: await_bytes(dqr.at[j, n], dq_s.at[n, j]))

        each(lent)
        return carry

    lax.fori_loop(0, nh, settle, 0)
    for half in range(2):
        each(lambda n: await_bytes(dqr.at[nh - 1, n, pl.ds(0, 2 * TILE)], dqh_s.at[n, half]))
    for a, out in enumerate((oq_ref, ok_ref, ov_ref)):
        await_bytes(out, out_r.at[a])


def hand_over(aq, ak, av, bq, bk, bv, out):
    copies = [pltpu.make_async_copy(a, b, out.at[n]) for n, (a, b) in enumerate(((aq, bq), (ak, bk), (av, bv)))]
    for copy in copies:
        copy.start()
    for copy in copies:
        copy.wait()


def local(queries, keys, values, out_grad, neighbours):
    nh = queries.shape[-1] // HD // 8
    tiles = (2, 2, 4, TILE // 4, HD)
    bf, f32 = jnp.bfloat16, jnp.float32
    dma = pltpu.SemaphoreType.DMA
    any_spec = pl.BlockSpec(memory_space=pl.ANY)
    shape = jax.ShapeDtypeStruct(queries.shape, bf)
    products = 5 * 512 * 1536 * HD * nh
    grads = pl.pallas_call(
        functools.partial(kernel, nh),
        out_shape=(pltpu.VMEM(queries.shape, bf),) * 3,
        in_specs=[any_spec] * 5,
        out_specs=[pl.BlockSpec(memory_space=pltpu.VMEM)] * 3,
        scratch_shapes=[
            pltpu.VMEM(neighbours.shape, jnp.int32),
            pltpu.VMEM((3, nh, 2) + tiles, bf),
            pltpu.VMEM((nh, 2) + tiles, bf),
            pltpu.VMEM((3, 2, 8, 256), f32),
            pltpu.VMEM((3, 2, 8, 256), f32),
            pltpu.VMEM((3, 6, 4, TILE, 256), f32),
            pltpu.VMEM((3, 6, 4, TILE, 256), f32),
            pltpu.VMEM((3, 6, 8, 256), f32),
            pltpu.VMEM((nh, 3, 8, 256), f32),
            pltpu.VMEM((nh, 2, 8, 256), f32),
            pltpu.VMEM((nh, 3, 8, 256), f32),
            pltpu.VMEM((4, TILE, HD), f32),
            pltpu.VMEM((4, TILE, HD), f32),
            pltpu.VMEM((nh, 3, 512, HD), bf),
            pltpu.VMEM((nh, 2, 512, HD), bf),
            pltpu.VMEM((nh, 512, HD), f32),
            pltpu.VMEM((nh, 3) + tiles, bf),
            dma((nh, 4)), dma((nh, 4)),
            dma((2, nh)), dma((2, nh)),
            dma((2, nh)), dma((2, nh)),
            dma((2, nh)), dma((2, nh)),
            dma((2, nh)), dma((2, nh)),
            dma((nh, 3)), dma((3,)),
            dma(()), dma(()),
            dma((2,)), dma((2,)),
            dma(()),
            dma((2, 2)), dma((2, 2)),
        ],
        compiler_params=pltpu.CompilerParams(
            collective_id=0, has_side_effects=True, vmem_limit_bytes=48 * 1024 * 1024
        ),
        cost_estimate=pl.CostEstimate(
            flops=2 * products, bytes_accessed=7 * 2 * queries.size, transcendentals=512 * 1536 * nh
        ),
        name="window_backward",
    )(*(pltpu.with_memory_space_constraint(a, pltpu.HBM) for a in (queries, keys, values, out_grad, neighbours)))
    return pl.pallas_call(
        hand_over,
        out_shape=(shape, shape, shape),
        in_specs=[pl.BlockSpec(memory_space=pltpu.VMEM)] * 3,
        out_specs=[any_spec] * 3,
        scratch_shapes=[dma((3,))],
        name="hand_over",
    )(*(pltpu.with_memory_space_constraint(a, pltpu.VMEM) for a in grads))


def solution(mesh):
    whole = P("frames", "rows", None, "heads", None)
    return jax.shard_map(
        local,
        mesh=mesh,
        in_specs=(whole, whole, whole, whole, P("frames", "rows", None, None)),
        out_specs=(whole, whole, whole),
        check_vma=False,
    )
```

```python
import functools

import jax
import jax.numpy as jnp
from jax import lax
from jax.experimental import pallas as pl
from jax.experimental.pallas import tpu as pltpu
from jax.sharding import PartitionSpec as P

MESH = pl.DeviceIdType.MESH
HD = 128
TILE = 128
NROWS = 16
LOG2E = 1.4426950408889634
NONE = -1e30
NT = (((1,), (1,)), ((), ()))
NN = (((1,), (0,)), ((), ()))
TN = (((0,), (0,)), ((), ()))


def dot(a, b, dims):
    return lax.dot_general(a, b, dims, preferred_element_type=jnp.float32)


def phase_a(s, j, p, qg, kv, bias, es, dps, ms, pst):
    scale = LOG2E * HD**-0.5

    def block(f, carry):
        i = 2 * s + f
        q = qg[s, j, 0, f].reshape(2 * TILE, HD)
        g = qg[s, j, 1, f].reshape(2 * TILE, HD)
        peaks, sums, prods = [], [], []
        for kt in range(4):
            k = kv[j, 0, kt // 2, kt % 2].reshape(TILE, HD)
            v = kv[j, 1, kt // 2, kt % 2].reshape(TILE, HD)
            st = dot(k, q, NT) * scale
            m = jnp.max(st, axis=0, keepdims=True)
            e = jnp.exp2(st - m)
            dp = dot(v, g, NT)
            es[p, i, kt] = e
            dps[p, i, kt] = dp
            mb = m + bias[s, 4 * f + kt : 4 * f + kt + 1, :]
            ms[p, i, kt : kt + 1, :] = mb
            peaks.append(mb)
            sums.append(jnp.sum(e, axis=0, keepdims=True))
            prods.append(jnp.sum(e * dp, axis=0, keepdims=True))
        top = functools.reduce(jnp.maximum, peaks)
        ws = [jnp.exp2(mb - top) for mb in peaks]
        total = sum(w * l for w, l in zip(ws, sums))
        pst[j, s, 2 * f : 2 * f + 1, :] = top + jnp.log2(total)
        pst[j, s, 2 * f + 1 : 2 * f + 2, :] = sum(w * d for w, d in zip(ws, prods)) / total
        return carry

    block(0, 0)
    block(1, 0)


def combine(j, pst, prc, fin):
    for f in range(2):
        rows = slice(2 * f, 2 * f + 2)
        parts = [pst[j, 1, rows], prc[j, 0, rows], prc[j, 1, rows]]
        top = functools.reduce(jnp.maximum, [x[0:1] for x in parts])
        ws = [jnp.exp2(x[0:1] - top) for x in parts]
        total = sum(ws)
        prod = sum(w * x[1:2] for w, x in zip(ws, parts))
        fin[j, 1, 2 * f : 2 * f + 1, :] = top + jnp.log2(total)
        fin[j, 1, 2 * f + 1 : 2 * f + 2, :] = prod / total


def phase_b(s, j, p, qg, kv, es, dps, ms, fin, dka, dva, dqs, dqf):
    scale = HD**-0.5

    def block(f, carry):
        i = 2 * s + f
        q = qg[s, j, 0, f].reshape(2 * TILE, HD)
        g = qg[s, j, 1, f].reshape(2 * TILE, HD)
        lse = fin[j, s, 2 * f : 2 * f + 1, :]
        delta = fin[j, s, 2 * f + 1 : 2 * f + 2, :]
        probs, grads = [], []
        for kt in range(4):
            r = jnp.exp2(ms[p, i, kt : kt + 1, :] - lse)
            prob = es[p, i, kt] * r
            ds = (prob * (dps[p, i, kt] - delta)).astype(jnp.bfloat16)
            probs.append(prob.astype(jnp.bfloat16))
            grads.append(ds)
        probs, grads = jnp.concatenate(probs), jnp.concatenate(grads)
        dva[...] += dot(probs, g, NN).reshape(dva.shape)
        dka[...] += dot(grads, q, NN).reshape(dka.shape)
        dq = dot(kv[j, 0].reshape(4 * TILE, HD), grads, TN).T * scale
        rows = pl.ds(pl.multiple_of(f * 2 * TILE, 2 * TILE), 2 * TILE)
        if isinstance(s, int):
            dqf[j, rows] = dq
        else:
            dqs[j, s, rows] = dq.astype(jnp.bfloat16)
        return carry

    block(0, 0)
    block(1, 0)


def kernel(nh, q_ref, k_ref, v_ref, g_ref, nb_hbm, oq_ref, ok_ref, ov_ref,
           nb_ref, qg, kv, tab, lent, bias, es, dps, ms, pst, prc, fin, dka, dva, dqs, dqr, dqf, ost,
           xin_s, xin_r, halo_s, halo_r, part_s, part_r, fin_s, fin_r, dq_s, dq_r, out_s, out_r,
           tab_s, tab_r, bias_s, bias_r, nb_s, dqh_s, dqh_r, early_r):
    f = lax.axis_index("frames")
    h = lax.axis_index("rows")
    x = lax.axis_index("heads")
    me = x * 2 + f
    beside = (f, jnp.maximum(h - 1, 0), x), (f, jnp.minimum(h + 1, NROWS - 1), x)
    held = h > 0, h < NROWS - 1

    def member(k):
        other = lax.rem(me + k, 8)
        return other, (other % 2, h, other // 2)

    near = pltpu.make_async_copy(nb_hbm, nb_ref, nb_s)
    near.start()
    barrier = pltpu.get_barrier_semaphore()
    for k in range(1, 8):
        pl.semaphore_signal(barrier, inc=1, device_id=member(k)[1], device_id_type=MESH)
    for n in range(2):

        @pl.when(held[n])
        def _():
            pl.semaphore_signal(barrier, inc=1, device_id=beside[n], device_id_type=MESH)

    pl.semaphore_wait(barrier, 7 + held[0].astype(jnp.int32) + held[1].astype(jnp.int32))

    def remote(src, dst, send, recv, device):
        return pltpu.make_async_remote_copy(
            src_ref=src, dst_ref=dst, send_sem=send, recv_sem=recv, device_id=device, device_id_type=MESH
        )

    def await_bytes(ref, sem):
        pltpu.make_async_copy(ref, ref, sem).wait()

    def each(action):
        for n in range(2):
            pl.when(held[n])(functools.partial(action, n))

    def lanes(owner, j):
        return pl.ds(pl.multiple_of((owner * nh + j) * HD, HD), HD)

    def enter(j, pair, skip=0):
        sides = ((q_ref, qg.at[1, j, 0]), (g_ref, qg.at[1, j, 1])), ((k_ref, kv.at[j, 0]), (v_ref, kv.at[j, 1]))
        for a, (src, dst) in list(enumerate(sides[pair]))[skip:]:
            to = dst.at[f, :, x]
            recv = xin_r.at[j, 2 * pair + a]
            pltpu.make_async_copy(src.at[0, 0, :, :, lanes(me, j)], to, recv).start()
            for k in range(1, 8):
                other, device = member(k)
                remote(src.at[0, 0, :, :, lanes(other, j)], to, xin_s.at[j, 2 * pair + a], recv, device).start()

    def enter_first():
        for c in range(2):
            to = qg.at[1, 0, 0, f, c, x]
            recv = xin_r.at[0, 0] if c else early_r
            pltpu.make_async_copy(q_ref.at[0, 0, c, :, lanes(me, 0)], to, recv).start()
            for k in range(1, 8):
                other, device = member(k)
                remote(q_ref.at[0, 0, c, :, lanes(other, 0)], to, xin_s.at[0, 0], recv, device).start()

    def leave(j, a, out):
        to = out.at[0, 0, :, :, lanes(me, j)]
        pltpu.make_async_copy(ost.at[j, a, f, :, x], to, out_r.at[a]).start()
        for k in range(1, 8):
            other, device = member(k)
            remote(ost.at[j, a, other % 2, :, other // 2], to, out_s.at[j, a], out_r.at[a], device).start()

    def blank(n):
        dqr[:, n] = jnp.zeros_like(dqr[:, n])
        prc[:, n] = jnp.full_like(prc[:, n], NONE)

    def enter_both(j, carry):
        pl.when(j < nh)(lambda: enter(j, 0))
        pl.when(j >= 1)(lambda: enter(j - 1, 1))
        return carry

    enter_first()
    enter(0, 0, 1)
    lax.fori_loop(1, nh + 1, enter_both, 0)

    def lend_first():
        for c in range(2):
            await_bytes(qg.at[1, 0, 0, :, c], xin_r.at[0, 0] if c else early_r)
            each(lambda n: remote(qg.at[1, 0, 0, :, c], qg.at[2 - 2 * n, 0, 0, :, c], halo_s.at[n, 0], halo_r.at[1 - n, 0], beside[n]).start())

    def lend_queries(j, skip=0):
        for a in range(skip, 2):
            await_bytes(qg.at[1, j, a], xin_r.at[j, a])
            each(lambda n: remote(qg.at[1, j, a], qg.at[2 - 2 * n, j, a], halo_s.at[n, j], halo_r.at[1 - n, j], beside[n]).start())

    def return_queries(j):
        each(lambda n: remote(dqs.at[j, 2 * n], dqr.at[j, 1 - n], dq_s.at[n, j], dq_r.at[1 - n, j], beside[n]).start())

    def return_half(half):
        rows = pl.ds(half * 2 * TILE, 2 * TILE)
        each(lambda n: remote(dqs.at[nh - 1, 2 * n, rows], dqr.at[nh - 1, 1 - n, rows], dqh_s.at[n, half], dqh_r.at[1 - n, half], beside[n]).start())

    def finish_half(half):
        j, rows = nh - 1, pl.ds(half * 2 * TILE, 2 * TILE)
        each(lambda n: await_bytes(dqr.at[j, n, rows], dqh_r.at[n, half]))
        total = dqf[j, rows] + dqr[j, 0, rows].astype(jnp.float32) + dqr[j, 1, rows].astype(jnp.float32)
        ost[j, 0, half] = total.astype(jnp.bfloat16).reshape(ost.shape[3:])
        to = oq_ref.at[0, 0, :, :, lanes(me, j)]

        def across(k):
            xk = lax.rem(x + k, 4)
            remote(ost.at[j, 0, half, :, xk], to, out_s.at[j, 0], out_r.at[0], (half, h, xk)).start()

        @pl.when(f == half)
        def _():
            pltpu.make_async_copy(ost.at[j, 0, half, :, x], to, out_r.at[0]).start()

        pl.when(f != half)(lambda: across(0))
        for k in range(1, 4):
            across(k)

    def finish_queries(j):
        each(lambda n: await_bytes(dqr.at[j, n], dq_r.at[n, j]))
        total = dqf[j] + dqr[j, 0].astype(jnp.float32) + dqr[j, 1].astype(jnp.float32)
        ost[j, 0] = total.astype(jnp.bfloat16).reshape(ost.shape[2:])
        leave(j, 0, oq_ref)

    def neighbours_of(action):
        def body(n, carry):
            ahead = jnp.where(n == 0, h - 1, h + 1)
            pl.when(jnp.logical_and(ahead >= 0, ahead < NROWS))(lambda: action(n, (f, ahead, x)))
            return carry

        lax.fori_loop(0, 2, body, 0)

    def weights_beside(j):
        def one(n, device):
            await_bytes(qg.at[2 * n, j], halo_r.at[n, j])
            phase_a(2 * n, j, lax.rem(j, 3), qg, kv, bias, es, dps, ms, pst)
            remote(pst.at[j, 2 * n], prc.at[j, 1 - n], part_s.at[n, j], part_r.at[1 - n, j], device).start()

        neighbours_of(one)

    def gradients(j):
        dka[...] = jnp.zeros_like(dka)
        dva[...] = jnp.zeros_like(dva)

        def one(n, device):
            await_bytes(fin.at[j, 2 * n], fin_r.at[n, j])
            phase_b(2 * n, j, lax.rem(j, 3), qg, kv, es, dps, ms, fin, dka, dva, dqs, dqf)

        neighbours_of(one)

        @pl.when(j == nh - 1)
        def _():
            return_half(0)
            return_half(1)

        phase_b(1, j, lax.rem(j, 3), qg, kv, es, dps, ms, fin, dka, dva, dqs, dqf)
        ost[j, 1] = (dka[...] * HD**-0.5).astype(jnp.bfloat16).reshape(ost.shape[2:])
        ost[j, 2] = dva[...].astype(jnp.bfloat16).reshape(ost.shape[2:])
        leave(j, 1, ok_ref)
        leave(j, 2, ov_ref)

    def step(t, carry):
        pl.when(t + 1 < nh)(lambda: lend_queries(t + 1))

        pl.when(t == nh - 1)(lambda: return_queries(0))

        @pl.when(t < nh)
        def _():
            for a in range(2):
                await_bytes(kv.at[t, a], xin_r.at[t, 2 + a])
            phase_a(1, t, lax.rem(t, 3), qg, kv, bias, es, dps, ms, pst)

        @pl.when(t < nh)
        def _():
            pl.when(t == 0)(lambda: each(lambda n: lend[n].wait_recv()))
            weights_beside(t)

        @pl.when(jnp.logical_and(t >= 1, t < nh + 1))
        def _():
            j = t - 1
            each(lambda n: await_bytes(prc.at[j, n], part_r.at[n, j]))
            combine(j, pst, prc, fin)
            each(lambda n: remote(fin.at[j, 1], fin.at[j, 2 - 2 * n], fin_s.at[n, j], fin_r.at[1 - n, j], beside[n]).start())

        pl.when(t == nh - 1)(lambda: return_queries(1))
        pl.when(t == nh)(lambda: return_queries(2))
        pl.when(t == nh)(lambda: finish_queries(0))
        pl.when(t >= 2)(lambda: gradients(t - 2))
        pl.when(t == nh)(lambda: return_queries(3))
        pl.when(t == nh)(lambda: finish_queries(1))

        return carry

    near.wait()
    for n, dr in enumerate((1, 0, -1)):
        row = h + dr
        inside = jnp.logical_and(row >= 0, row < NROWS)
        for kt in range(4):
            wanted = jnp.where(inside, (kt // 2 * NROWS + row) * 2 + kt % 2, -2)
            for c in range(2):
                found = jnp.where(nb_ref[0, 0, c : c + 1, :] == wanted, 0.0, NONE)
                found = jnp.max(found, axis=-1, keepdims=True)
                tab[n, f, kt : kt + 1, c * TILE : (c + 1) * TILE] = jnp.broadcast_to(found, (1, TILE))
    swap = remote(tab.at[:, f], tab.at[:, f], tab_s, tab_r, (1 - f, h, x))
    swap.start()

    lend_first()
    lend_queries(0, 1)
    swap.wait()
    for g in range(2):
        lent[:, 4 * g : 4 * g + 4, :] = tab[:, g]
    bias[1] = lent[1]
    lend = [remote(lent.at[2 * n], bias.at[2 * n], bias_s.at[n], bias_r.at[n], beside[1 - n]) for n in range(2)]
    each(lambda n: lend[1 - n].start())

    @pl.when(h == 0)
    def _():
        blank(0)

    @pl.when(h == NROWS - 1)
    def _():
        blank(1)

    lax.fori_loop(0, nh + 2, step, 0)
    lax.fori_loop(2, nh - 1, lambda j, c: (finish_queries(j), c)[1], 0)
    finish_half(0)
    finish_half(1)

    each(lambda n: lend[1 - n].wait_send())

    def settle(j, carry):
        sent = dqs.at[j, 0, pl.ds(0, 7 * TILE // 2)]
        for a in range(4):
            await_bytes(sent, xin_s.at[j, a])
        for a in range(3):
            await_bytes(sent, out_s.at[j, a])

        def settle_beside(n):
            await_bytes(qg.at[1, j], halo_s.at[n, j])
            await_bytes(prc.at[j, n], part_s.at[n, j])
            await_bytes(prc.at[j, n], fin_s.at[n, j])
            pl.when(j < nh - 1)(lambda: await_bytes(dqr.at[j, n], dq_s.at[n, j]))

        each(settle_beside)
        return carry

    lax.fori_loop(0, nh, settle, 0)
    for half in range(2):
        each(lambda n: await_bytes(dqr.at[nh - 1, n, pl.ds(0, 2 * TILE)], dqh_s.at[n, half]))
    for a, out in enumerate((oq_ref, ok_ref, ov_ref)):
        await_bytes(out, out_r.at[a])


def hand_over(aq, ak, av, bq, bk, bv, out):
    copies = [pltpu.make_async_copy(a, b, out.at[n]) for n, (a, b) in enumerate(((aq, bq), (ak, bk), (av, bv)))]
    for copy in copies:
        copy.start()
    for copy in copies:
        copy.wait()


def local(queries, keys, values, out_grad, neighbours):
    nh = queries.shape[-1] // HD // 8
    tiles = (2, 2, 4, TILE // 4, HD)
    bf, f32 = jnp.bfloat16, jnp.float32
    dma = pltpu.SemaphoreType.DMA
    any_spec = pl.BlockSpec(memory_space=pl.ANY)
    shape = jax.ShapeDtypeStruct(queries.shape, bf)
    products = 5 * 512 * 1536 * HD * nh
    grads = pl.pallas_call(
        functools.partial(kernel, nh),
        out_shape=(pltpu.VMEM(queries.shape, bf),) * 3,
        in_specs=[any_spec] * 5,
        out_specs=[pl.BlockSpec(memory_space=pltpu.VMEM)] * 3,
        scratch_shapes=[
            pltpu.VMEM(neighbours.shape, jnp.int32),
            pltpu.VMEM((3, nh, 2) + tiles, bf),
            pltpu.VMEM((nh, 2) + tiles, bf),
            pltpu.VMEM((3, 2, 4, 256), f32),
            pltpu.VMEM((3, 8, 256), f32),
            pltpu.VMEM((3, 8, 256), f32),
            pltpu.VMEM((3, 6, 4, TILE, 256), f32),
            pltpu.VMEM((3, 6, 4, TILE, 256), f32),
            pltpu.VMEM((3, 6, 8, 256), f32),
            pltpu.VMEM((nh, 3, 4, 256), f32),
            pltpu.VMEM((nh, 2, 4, 256), f32),
            pltpu.VMEM((nh, 3, 4, 256), f32),
            pltpu.VMEM((4, TILE, HD), f32),
            pltpu.VMEM((4, TILE, HD), f32),
            pltpu.VMEM((nh, 3, 512, HD), bf),
            pltpu.VMEM((nh, 2, 512, HD), bf),
            pltpu.VMEM((nh, 512, HD), f32),
            pltpu.VMEM((nh, 3) + tiles, bf),
            dma((nh, 4)), dma((nh, 4)),
            dma((2, nh)), dma((2, nh)),
            dma((2, nh)), dma((2, nh)),
            dma((2, nh)), dma((2, nh)),
            dma((2, nh)), dma((2, nh)),
            dma((nh, 3)), dma((3,)),
            dma(()), dma(()),
            dma((2,)), dma((2,)),
            dma(()),
            dma((2, 2)), dma((2, 2)),
            dma(()),
        ],
        compiler_params=pltpu.CompilerParams(
            collective_id=0, has_side_effects=True, vmem_limit_bytes=48 * 1024 * 1024
        ),
        cost_estimate=pl.CostEstimate(
            flops=2 * products, bytes_accessed=7 * 2 * queries.size, transcendentals=512 * 1536 * nh
        ),
        name="window_backward",
    )(*(pltpu.with_memory_space_constraint(a, pltpu.HBM) for a in (queries, keys, values, out_grad, neighbours)))
    return pl.pallas_call(
        hand_over,
        out_shape=(shape, shape, shape),
        in_specs=[pl.BlockSpec(memory_space=pltpu.VMEM)] * 3,
        out_specs=[any_spec] * 3,
        scratch_shapes=[dma((3,))],
        name="hand_over",
    )(*(pltpu.with_memory_space_constraint(a, pltpu.VMEM) for a in grads))


def solution(mesh):
    whole = P("frames", "rows", None, "heads", None)
    return jax.shard_map(
        local,
        mesh=mesh,
        in_specs=(whole, whole, whole, whole, P("frames", "rows", None, None)),
        out_specs=(whole, whole, whole),
        check_vma=False,
    )
```

```python
import functools

import jax
import jax.numpy as jnp
from jax import lax
from jax.experimental import pallas as pl
from jax.experimental.pallas import tpu as pltpu
from jax.sharding import PartitionSpec as P

MESH = pl.DeviceIdType.MESH
HD = 128
TILE = 128
NROWS = 16
LOG2E = 1.4426950408889634
NONE = -1e30
NT = (((1,), (1,)), ((), ()))
NN = (((1,), (0,)), ((), ()))
TN = (((0,), (0,)), ((), ()))


def dot(a, b, dims):
    return lax.dot_general(a, b, dims, preferred_element_type=jnp.float32)


def phase_a(s, j, p, qg, kv, bias, es, dps, ms, pst):
    scale = LOG2E * HD**-0.5

    def block(f, carry):
        i = 2 * s + f
        q = qg[s, j, 0, f].reshape(2 * TILE, HD)
        g = qg[s, j, 1, f].reshape(2 * TILE, HD)
        peaks, sums, prods = [], [], []
        for kt in range(4):
            k = kv[j, 0, kt // 2, kt % 2].reshape(TILE, HD)
            v = kv[j, 1, kt // 2, kt % 2].reshape(TILE, HD)
            st = dot(k, q, NT) * scale
            m = jnp.max(st, axis=0, keepdims=True)
            e = jnp.exp2(st - m)
            dp = dot(v, g, NT)
            es[p, i, kt] = e
            dps[p, i, kt] = dp
            mb = m + bias[s, 4 * f + kt : 4 * f + kt + 1, :]
            ms[p, i, kt : kt + 1, :] = mb
            peaks.append(mb)
            sums.append(jnp.sum(e, axis=0, keepdims=True))
            prods.append(jnp.sum(e * dp, axis=0, keepdims=True))
        top = functools.reduce(jnp.maximum, peaks)
        ws = [jnp.exp2(mb - top) for mb in peaks]
        total = sum(w * l for w, l in zip(ws, sums))
        pst[j, s, 2 * f : 2 * f + 1, :] = top + jnp.log2(total)
        pst[j, s, 2 * f + 1 : 2 * f + 2, :] = sum(w * d for w, d in zip(ws, prods)) / total
        return carry

    block(0, 0)
    block(1, 0)


def combine(j, pst, prc, fin):
    for f in range(2):
        rows = slice(2 * f, 2 * f + 2)
        parts = [pst[j, 1, rows], prc[j, 0, rows], prc[j, 1, rows]]
        top = functools.reduce(jnp.maximum, [x[0:1] for x in parts])
        ws = [jnp.exp2(x[0:1] - top) for x in parts]
        total = sum(ws)
        prod = sum(w * x[1:2] for w, x in zip(ws, parts))
        fin[j, 1, 2 * f : 2 * f + 1, :] = top + jnp.log2(total)
        fin[j, 1, 2 * f + 1 : 2 * f + 2, :] = prod / total


def phase_b(s, j, p, qg, kv, es, dps, ms, fin, dka, dva, dqs, dqf):
    scale = HD**-0.5

    def block(f, carry):
        i = 2 * s + f
        q = qg[s, j, 0, f].reshape(2 * TILE, HD)
        g = qg[s, j, 1, f].reshape(2 * TILE, HD)
        lse = fin[j, s, 2 * f : 2 * f + 1, :]
        delta = fin[j, s, 2 * f + 1 : 2 * f + 2, :]
        probs, grads = [], []
        for kt in range(4):
            r = jnp.exp2(ms[p, i, kt : kt + 1, :] - lse)
            prob = es[p, i, kt] * r
            ds = (prob * (dps[p, i, kt] - delta)).astype(jnp.bfloat16)
            probs.append(prob.astype(jnp.bfloat16))
            grads.append(ds)
        probs, grads = jnp.concatenate(probs), jnp.concatenate(grads)
        dva[...] += dot(probs, g, NN).reshape(dva.shape)
        dka[...] += dot(grads, q, NN).reshape(dka.shape)
        dq = dot(kv[j, 0].reshape(4 * TILE, HD), grads, TN).T * scale
        rows = pl.ds(pl.multiple_of(f * 2 * TILE, 2 * TILE), 2 * TILE)
        if isinstance(s, int):
            dqf[j, rows] = dq
        else:
            dqs[j, s, rows] = dq.astype(jnp.bfloat16)
        return carry

    block(0, 0)
    block(1, 0)


def kernel(nh, q_ref, k_ref, v_ref, g_ref, nb_hbm, oq_ref, ok_ref, ov_ref,
           nb_ref, qg, kv, tab, lent, bias, es, dps, ms, pst, prc, fin, dka, dva, dqs, dqr, dqf, ost,
           xin_s, xin_r, halo_s, halo_r, part_s, part_r, fin_s, fin_r, dq_s, dq_r, out_s, out_r,
           tab_s, tab_r, bias_s, bias_r, nb_s, dqh_s, dqh_r, early_r):
    f = lax.axis_index("frames")
    h = lax.axis_index("rows")
    x = lax.axis_index("heads")
    me = x * 2 + f
    beside = (f, jnp.maximum(h - 1, 0), x), (f, jnp.minimum(h + 1, NROWS - 1), x)
    held = h > 0, h < NROWS - 1

    def member(k):
        other = lax.rem(me + k, 8)
        return other, (other % 2, h, other // 2)

    near = pltpu.make_async_copy(nb_hbm, nb_ref, nb_s)
    near.start()
    barrier = pltpu.get_barrier_semaphore()
    for k in range(1, 8):
        pl.semaphore_signal(barrier, inc=1, device_id=member(k)[1], device_id_type=MESH)
    for n in range(2):

        @pl.when(held[n])
        def _():
            pl.semaphore_signal(barrier, inc=1, device_id=beside[n], device_id_type=MESH)

    pl.semaphore_wait(barrier, 7 + held[0].astype(jnp.int32) + held[1].astype(jnp.int32))

    def remote(src, dst, send, recv, device):
        return pltpu.make_async_remote_copy(
            src_ref=src, dst_ref=dst, send_sem=send, recv_sem=recv, device_id=device, device_id_type=MESH
        )

    def await_bytes(ref, sem):
        pltpu.make_async_copy(ref, ref, sem).wait()

    def each(action):
        for n in range(2):
            pl.when(held[n])(functools.partial(action, n))

    def lanes(owner, j):
        return pl.ds(pl.multiple_of((owner * nh + j) * HD, HD), HD)

    def enter(j, pair, skip=0):
        sides = ((q_ref, qg.at[1, j, 0]), (g_ref, qg.at[1, j, 1])), ((k_ref, kv.at[j, 0]), (v_ref, kv.at[j, 1]))
        for a, (src, dst) in list(enumerate(sides[pair]))[skip:]:
            to = dst.at[f, :, x]
            recv = xin_r.at[j, 2 * pair + a]
            pltpu.make_async_copy(src.at[0, 0, :, :, lanes(me, j)], to, recv).start()
            for k in range(1, 8):
                other, device = member(k)
                remote(src.at[0, 0, :, :, lanes(other, j)], to, xin_s.at[j, 2 * pair + a], recv, device).start()

    def enter_first():
        for c in range(2):
            to = qg.at[1, 0, 0, f, c, x]
            recv = xin_r.at[0, 0] if c else early_r
            pltpu.make_async_copy(q_ref.at[0, 0, c, :, lanes(me, 0)], to, recv).start()
            for k in range(1, 8):
                other, device = member(k)
                remote(q_ref.at[0, 0, c, :, lanes(other, 0)], to, xin_s.at[0, 0], recv, device).start()

    def leave(j, a, out):
        to = out.at[0, 0, :, :, lanes(me, j)]
        pltpu.make_async_copy(ost.at[j, a, f, :, x], to, out_r.at[a]).start()
        for k in range(1, 8):
            other, device = member(k)
            remote(ost.at[j, a, other % 2, :, other // 2], to, out_s.at[j, a], out_r.at[a], device).start()

    def blank(n):
        dqr[:, n] = jnp.zeros_like(dqr[:, n])
        prc[:, n] = jnp.full_like(prc[:, n], NONE)

    def enter_both(j, carry):
        pl.when(j < nh)(lambda: enter(j, 0))
        pl.when(j >= 1)(lambda: enter(j - 1, 1))
        return carry

    enter_first()
    enter(0, 0, 1)
    lax.fori_loop(1, nh + 1, enter_both, 0)

    def lend_first():
        for c in range(2):
            await_bytes(qg.at[1, 0, 0, :, c], xin_r.at[0, 0] if c else early_r)
            each(lambda n: remote(qg.at[1, 0, 0, :, c], qg.at[2 - 2 * n, 0, 0, :, c], halo_s.at[n, 0], halo_r.at[1 - n, 0], beside[n]).start())

    def lend_queries(j, start, stop):
        for a in range(start, stop):
            await_bytes(qg.at[1, j, a], xin_r.at[j, a])
            each(lambda n: remote(qg.at[1, j, a], qg.at[2 - 2 * n, j, a], halo_s.at[n, j], halo_r.at[1 - n, j], beside[n]).start())

    def return_queries(j):
        each(lambda n: remote(dqs.at[j, 2 * n], dqr.at[j, 1 - n], dq_s.at[n, j], dq_r.at[1 - n, j], beside[n]).start())

    def return_half(half):
        rows = pl.ds(half * 2 * TILE, 2 * TILE)
        each(lambda n: remote(dqs.at[nh - 1, 2 * n, rows], dqr.at[nh - 1, 1 - n, rows], dqh_s.at[n, half], dqh_r.at[1 - n, half], beside[n]).start())

    def finish_half(half):
        j, rows = nh - 1, pl.ds(half * 2 * TILE, 2 * TILE)
        each(lambda n: await_bytes(dqr.at[j, n, rows], dqh_r.at[n, half]))
        total = dqf[j, rows] + dqr[j, 0, rows].astype(jnp.float32) + dqr[j, 1, rows].astype(jnp.float32)
        ost[j, 0, half] = total.astype(jnp.bfloat16).reshape(ost.shape[3:])
        to = oq_ref.at[0, 0, :, :, lanes(me, j)]

        def across(k):
            xk = lax.rem(x + k, 4)
            remote(ost.at[j, 0, half, :, xk], to, out_s.at[j, 0], out_r.at[0], (half, h, xk)).start()

        @pl.when(f == half)
        def _():
            pltpu.make_async_copy(ost.at[j, 0, half, :, x], to, out_r.at[0]).start()

        pl.when(f != half)(lambda: across(0))
        for k in range(1, 4):
            across(k)

    def finish_queries(j):
        each(lambda n: await_bytes(dqr.at[j, n], dq_r.at[n, j]))
        total = dqf[j] + dqr[j, 0].astype(jnp.float32) + dqr[j, 1].astype(jnp.float32)
        ost[j, 0] = total.astype(jnp.bfloat16).reshape(ost.shape[2:])
        leave(j, 0, oq_ref)

    def neighbours_of(action):
        def body(n, carry):
            ahead = jnp.where(n == 0, h - 1, h + 1)
            pl.when(jnp.logical_and(ahead >= 0, ahead < NROWS))(lambda: action(n, (f, ahead, x)))
            return carry

        lax.fori_loop(0, 2, body, 0)

    def weights_beside(j):
        def one(n, device):
            await_bytes(qg.at[2 * n, j], halo_r.at[n, j])
            phase_a(2 * n, j, lax.rem(j, 3), qg, kv, bias, es, dps, ms, pst)
            remote(pst.at[j, 2 * n], prc.at[j, 1 - n], part_s.at[n, j], part_r.at[1 - n, j], device).start()

        neighbours_of(one)

    def gradients(j):
        dka[...] = jnp.zeros_like(dka)
        dva[...] = jnp.zeros_like(dva)

        def one(n, device):
            await_bytes(fin.at[j, 2 * n], fin_r.at[n, j])
            phase_b(2 * n, j, lax.rem(j, 3), qg, kv, es, dps, ms, fin, dka, dva, dqs, dqf)

        neighbours_of(one)

        @pl.when(j == nh - 1)
        def _():
            return_half(0)
            return_half(1)

        phase_b(1, j, lax.rem(j, 3), qg, kv, es, dps, ms, fin, dka, dva, dqs, dqf)
        ost[j, 1] = (dka[...] * HD**-0.5).astype(jnp.bfloat16).reshape(ost.shape[2:])
        ost[j, 2] = dva[...].astype(jnp.bfloat16).reshape(ost.shape[2:])
        leave(j, 1, ok_ref)
        leave(j, 2, ov_ref)

    def step(t, carry):
        pl.when(t + 1 < nh)(lambda: lend_queries(t + 1, 0, 1))

        @pl.when(t >= nh - 2)
        def _():
            low = jnp.where(t < nh, t - nh + 2, t - 2)
            high = jnp.where(t == nh - 2, 1, t - 1)
            lax.fori_loop(low, high, lambda j, c: (gradients(j), c)[1], 0)

        @pl.when(jnp.logical_and(t >= 1, t < nh + 1))
        def _():
            j = t - 1
            each(lambda n: await_bytes(prc.at[j, n], part_r.at[n, j]))
            combine(j, pst, prc, fin)
            each(lambda n: remote(fin.at[j, 1], fin.at[j, 2 - 2 * n], fin_s.at[n, j], fin_r.at[1 - n, j], beside[n]).start())

        pl.when(t == nh - 1)(lambda: return_queries(1))
        pl.when(t + 1 < nh)(lambda: lend_queries(t + 1, 1, 2))

        @pl.when(t < nh)
        def _():
            for a in range(2):
                await_bytes(kv.at[t, a], xin_r.at[t, 2 + a])
            phase_a(1, t, lax.rem(t, 3), qg, kv, bias, es, dps, ms, pst)
            pl.when(t == 0)(lambda: each(lambda n: lend[n].wait_recv()))
            weights_beside(t)

        pl.when(t == nh - 2)(lambda: return_queries(0))
        pl.when(t == nh - 1)(lambda: return_queries(2))
        pl.when(t == nh)(lambda: return_queries(3))

        @pl.when(jnp.logical_or(t == nh - 1, t == nh))
        def _():
            lax.fori_loop(t - nh + 1, 2 * (t - nh) + 3, lambda j, c: (finish_queries(j), c)[1], 0)

        return carry

    near.wait()
    for n, dr in enumerate((1, 0, -1)):
        row = h + dr
        inside = jnp.logical_and(row >= 0, row < NROWS)
        for kt in range(4):
            wanted = jnp.where(inside, (kt // 2 * NROWS + row) * 2 + kt % 2, -2)
            for c in range(2):
                found = jnp.where(nb_ref[0, 0, c : c + 1, :] == wanted, 0.0, NONE)
                found = jnp.max(found, axis=-1, keepdims=True)
                tab[n, f, kt : kt + 1, c * TILE : (c + 1) * TILE] = jnp.broadcast_to(found, (1, TILE))
    swap = remote(tab.at[:, f], tab.at[:, f], tab_s, tab_r, (1 - f, h, x))
    swap.start()

    lend_first()
    lend_queries(0, 1, 2)
    swap.wait()
    for g in range(2):
        lent[:, 4 * g : 4 * g + 4, :] = tab[:, g]
    bias[1] = lent[1]
    lend = [remote(lent.at[2 * n], bias.at[2 * n], bias_s.at[n], bias_r.at[n], beside[1 - n]) for n in range(2)]
    each(lambda n: lend[1 - n].start())

    @pl.when(h == 0)
    def _():
        blank(0)

    @pl.when(h == NROWS - 1)
    def _():
        blank(1)

    lax.fori_loop(0, nh + 2, step, 0)
    finish_queries(3)
    finish_half(0)
    finish_half(1)

    each(lambda n: lend[1 - n].wait_send())

    def settle(j, carry):
        sent = dqs.at[j, 0, pl.ds(0, 7 * TILE // 2)]
        for a in range(4):
            await_bytes(sent, xin_s.at[j, a])
        for a in range(3):
            await_bytes(sent, out_s.at[j, a])

        def settle_beside(n):
            await_bytes(qg.at[1, j], halo_s.at[n, j])
            await_bytes(prc.at[j, n], part_s.at[n, j])
            await_bytes(prc.at[j, n], fin_s.at[n, j])
            pl.when(j < nh - 1)(lambda: await_bytes(dqr.at[j, n], dq_s.at[n, j]))

        each(settle_beside)
        return carry

    lax.fori_loop(0, nh, settle, 0)
    for half in range(2):
        each(lambda n: await_bytes(dqr.at[nh - 1, n, pl.ds(0, 2 * TILE)], dqh_s.at[n, half]))
    for a, out in enumerate((oq_ref, ok_ref, ov_ref)):
        await_bytes(out, out_r.at[a])


def hand_over(aq, ak, av, bq, bk, bv, out):
    copies = [pltpu.make_async_copy(a, b, out.at[n]) for n, (a, b) in enumerate(((aq, bq), (ak, bk), (av, bv)))]
    for copy in copies:
        copy.start()
    for copy in copies:
        copy.wait()


def local(queries, keys, values, out_grad, neighbours):
    nh = queries.shape[-1] // HD // 8
    tiles = (2, 2, 4, TILE // 4, HD)
    bf, f32 = jnp.bfloat16, jnp.float32
    dma = pltpu.SemaphoreType.DMA
    any_spec = pl.BlockSpec(memory_space=pl.ANY)
    shape = jax.ShapeDtypeStruct(queries.shape, bf)
    products = 5 * 512 * 1536 * HD * nh
    grads = pl.pallas_call(
        functools.partial(kernel, nh),
        out_shape=(pltpu.VMEM(queries.shape, bf),) * 3,
        in_specs=[any_spec] * 5,
        out_specs=[pl.BlockSpec(memory_space=pltpu.VMEM)] * 3,
        scratch_shapes=[
            pltpu.VMEM(neighbours.shape, jnp.int32),
            pltpu.VMEM((3, nh, 2) + tiles, bf),
            pltpu.VMEM((nh, 2) + tiles, bf),
            pltpu.VMEM((3, 2, 4, 256), f32),
            pltpu.VMEM((3, 8, 256), f32),
            pltpu.VMEM((3, 8, 256), f32),
            pltpu.VMEM((3, 6, 4, TILE, 256), f32),
            pltpu.VMEM((3, 6, 4, TILE, 256), f32),
            pltpu.VMEM((3, 6, 8, 256), f32),
            pltpu.VMEM((nh, 3, 4, 256), f32),
            pltpu.VMEM((nh, 2, 4, 256), f32),
            pltpu.VMEM((nh, 3, 4, 256), f32),
            pltpu.VMEM((4, TILE, HD), f32),
            pltpu.VMEM((4, TILE, HD), f32),
            pltpu.VMEM((nh, 3, 512, HD), bf),
            pltpu.VMEM((nh, 2, 512, HD), bf),
            pltpu.VMEM((nh, 512, HD), f32),
            pltpu.VMEM((nh, 3) + tiles, bf),
            dma((nh, 4)), dma((nh, 4)),
            dma((2, nh)), dma((2, nh)),
            dma((2, nh)), dma((2, nh)),
            dma((2, nh)), dma((2, nh)),
            dma((2, nh)), dma((2, nh)),
            dma((nh, 3)), dma((3,)),
            dma(()), dma(()),
            dma((2,)), dma((2,)),
            dma(()),
            dma((2, 2)), dma((2, 2)),
            dma(()),
        ],
        compiler_params=pltpu.CompilerParams(
            collective_id=0, has_side_effects=True, vmem_limit_bytes=48 * 1024 * 1024
        ),
        cost_estimate=pl.CostEstimate(
            flops=2 * products, bytes_accessed=7 * 2 * queries.size, transcendentals=512 * 1536 * nh
        ),
        name="window_backward",
    )(*(pltpu.with_memory_space_constraint(a, pltpu.HBM) for a in (queries, keys, values, out_grad, neighbours)))
    return pl.pallas_call(
        hand_over,
        out_shape=(shape, shape, shape),
        in_specs=[pl.BlockSpec(memory_space=pltpu.VMEM)] * 3,
        out_specs=[any_spec] * 3,
        scratch_shapes=[dma((3,))],
        name="hand_over",
    )(*(pltpu.with_memory_space_constraint(a, pltpu.VMEM) for a in grads))


def solution(mesh):
    whole = P("frames", "rows", None, "heads", None)
    return jax.shard_map(
        local,
        mesh=mesh,
        in_specs=(whole, whole, whole, whole, P("frames", "rows", None, None)),
        out_specs=(whole, whole, whole),
        check_vma=False,
    )
```

```python
import functools

import jax
import jax.numpy as jnp
from jax import lax
from jax.experimental import pallas as pl
from jax.experimental.pallas import tpu as pltpu
from jax.sharding import PartitionSpec as P

MESH = pl.DeviceIdType.MESH
HD = 128
TILE = 128
NROWS = 16
LOG2E = 1.4426950408889634
NONE = -1e30
NT = (((1,), (1,)), ((), ()))
NN = (((1,), (0,)), ((), ()))
TN = (((0,), (0,)), ((), ()))


def dot(a, b, dims):
    return lax.dot_general(a, b, dims, preferred_element_type=jnp.float32)


def phase_a(s, j, p, qg, kv, bias, es, dps, ms, pst):
    scale = LOG2E * HD**-0.5

    def block(f, carry):
        i = 2 * s + f
        q = qg[s, j, 0, f].reshape(2 * TILE, HD)
        g = qg[s, j, 1, f].reshape(2 * TILE, HD)
        peaks, sums, prods = [], [], []
        for kt in range(4):
            k = kv[j, 0, kt // 2, kt % 2].reshape(TILE, HD)
            v = kv[j, 1, kt // 2, kt % 2].reshape(TILE, HD)
            st = dot(k, q, NT) * scale
            m = jnp.max(st, axis=0, keepdims=True)
            e = jnp.exp2(st - m)
            dp = dot(v, g, NT)
            es[p, i, kt] = e
            dps[p, i, kt] = dp
            mb = m + bias[s, 4 * f + kt : 4 * f + kt + 1, :]
            ms[p, i, kt : kt + 1, :] = mb
            peaks.append(mb)
            sums.append(jnp.sum(e, axis=0, keepdims=True))
            prods.append(jnp.sum(e * dp, axis=0, keepdims=True))
        top = functools.reduce(jnp.maximum, peaks)
        ws = [jnp.exp2(mb - top) for mb in peaks]
        total = sum(w * l for w, l in zip(ws, sums))
        pst[j, s, 2 * f : 2 * f + 1, :] = top + jnp.log2(total)
        pst[j, s, 2 * f + 1 : 2 * f + 2, :] = sum(w * d for w, d in zip(ws, prods)) / total
        return carry

    block(0, 0)
    block(1, 0)


def combine(j, pst, prc, fin):
    for f in range(2):
        rows = slice(2 * f, 2 * f + 2)
        parts = [pst[j, 1, rows], prc[j, 0, rows], prc[j, 1, rows]]
        top = functools.reduce(jnp.maximum, [x[0:1] for x in parts])
        ws = [jnp.exp2(x[0:1] - top) for x in parts]
        total = sum(ws)
        prod = sum(w * x[1:2] for w, x in zip(ws, parts))
        fin[j, 1, 2 * f : 2 * f + 1, :] = top + jnp.log2(total)
        fin[j, 1, 2 * f + 1 : 2 * f + 2, :] = prod / total


def phase_b(s, j, p, qg, kv, es, dps, ms, fin, dka, dva, dqs, dqf):
    scale = HD**-0.5

    def block(f, carry):
        i = 2 * s + f
        q = qg[s, j, 0, f].reshape(2 * TILE, HD)
        g = qg[s, j, 1, f].reshape(2 * TILE, HD)
        lse = fin[j, s, 2 * f : 2 * f + 1, :]
        delta = fin[j, s, 2 * f + 1 : 2 * f + 2, :]
        probs, grads = [], []
        for kt in range(4):
            r = jnp.exp2(ms[p, i, kt : kt + 1, :] - lse)
            prob = es[p, i, kt] * r
            ds = (prob * (dps[p, i, kt] - delta)).astype(jnp.bfloat16)
            probs.append(prob.astype(jnp.bfloat16))
            grads.append(ds)
        probs, grads = jnp.concatenate(probs), jnp.concatenate(grads)
        dva[...] += dot(probs, g, NN).reshape(dva.shape)
        dka[...] += dot(grads, q, NN).reshape(dka.shape)
        dq = dot(kv[j, 0].reshape(4 * TILE, HD), grads, TN).T * scale
        rows = pl.ds(pl.multiple_of(f * 2 * TILE, 2 * TILE), 2 * TILE)
        if isinstance(s, int):
            dqf[j, rows] = dq
        else:
            dqs[j, s, rows] = dq.astype(jnp.bfloat16)
        return carry

    block(0, 0)
    block(1, 0)


def kernel(nh, q_ref, k_ref, v_ref, g_ref, nb_hbm, oq_ref, ok_ref, ov_ref,
           nb_ref, qg, kv, tab, lent, bias, es, dps, ms, pst, prc, fin, dka, dva, dqs, dqr, dqf, ost,
           xin_s, xin_r, halo_s, halo_r, part_s, part_r, fin_s, fin_r, dq_s, dq_r, out_s, out_r,
           tab_s, tab_r, bias_s, bias_r, nb_s, dqh_s, dqh_r, early_r):
    f = lax.axis_index("frames")
    h = lax.axis_index("rows")
    x = lax.axis_index("heads")
    me = x * 2 + f
    beside = (f, jnp.maximum(h - 1, 0), x), (f, jnp.minimum(h + 1, NROWS - 1), x)
    held = h > 0, h < NROWS - 1

    def member(k):
        across, other_core = ((1, 0), (3, 0), (2, 0), (1, 1), (3, 1), (2, 1), (0, 1))[k - 1]
        peer, core = lax.rem(x + across, 4), lax.rem(f + other_core, 2)
        return peer * 2 + core, (core, h, peer)

    barrier = pltpu.get_barrier_semaphore()
    for k in range(1, 8):
        pl.semaphore_signal(barrier, inc=1, device_id=member(k)[1], device_id_type=MESH)
    for n in range(2):

        @pl.when(held[n])
        def _():
            pl.semaphore_signal(barrier, inc=1, device_id=beside[n], device_id_type=MESH)

    near = pltpu.make_async_copy(nb_hbm, nb_ref, nb_s)
    near.start()
    pl.semaphore_wait(barrier, 7 + held[0].astype(jnp.int32) + held[1].astype(jnp.int32))

    def remote(src, dst, send, recv, device):
        return pltpu.make_async_remote_copy(
            src_ref=src, dst_ref=dst, send_sem=send, recv_sem=recv, device_id=device, device_id_type=MESH
        )

    def await_bytes(ref, sem):
        pltpu.make_async_copy(ref, ref, sem).wait()

    def each(action):
        for n in range(2):
            pl.when(held[n])(functools.partial(action, n))

    def lanes(owner, j):
        return pl.ds(pl.multiple_of((owner * nh + j) * HD, HD), HD)

    def enter(j, pair, skip=0):
        sides = ((q_ref, qg.at[1, j, 0]), (g_ref, qg.at[1, j, 1])), ((k_ref, kv.at[j, 0]), (v_ref, kv.at[j, 1]))
        for a, (src, dst) in list(enumerate(sides[pair]))[skip:]:
            to = dst.at[f, :, x]
            recv = xin_r.at[j, 2 * pair + a]
            pltpu.make_async_copy(src.at[0, 0, :, :, lanes(me, j)], to, recv).start()
            for k in range(1, 8):
                other, device = member(k)
                remote(src.at[0, 0, :, :, lanes(other, j)], to, xin_s.at[j, 2 * pair + a], recv, device).start()

    def enter_first():
        for c in range(2):
            to = qg.at[1, 0, 0, f, c, x]
            recv = xin_r.at[0, 0] if c else early_r
            pltpu.make_async_copy(q_ref.at[0, 0, c, :, lanes(me, 0)], to, recv).start()
            for k in range(1, 8):
                other, device = member(k)
                remote(q_ref.at[0, 0, c, :, lanes(other, 0)], to, xin_s.at[0, 0], recv, device).start()

    def leave(j, a, out):
        to = out.at[0, 0, :, :, lanes(me, j)]
        pltpu.make_async_copy(ost.at[j, a, f, :, x], to, out_r.at[a]).start()
        for k in range(1, 8):
            other, device = member(k)
            remote(ost.at[j, a, other % 2, :, other // 2], to, out_s.at[j, a], out_r.at[a], device).start()

    def blank(n):
        dqr[:, n] = jnp.zeros_like(dqr[:, n])
        prc[:, n] = jnp.full_like(prc[:, n], NONE)

    def enter_both(j, carry):
        pl.when(j < nh)(lambda: enter(j, 0))
        pl.when(j >= 1)(lambda: enter(j - 1, 1))
        return carry

    enter_first()
    enter(0, 0, 1)
    lax.fori_loop(1, nh + 1, enter_both, 0)

    def lend_first():
        for c in range(2):
            await_bytes(qg.at[1, 0, 0, :, c], xin_r.at[0, 0] if c else early_r)
            each(lambda n: remote(qg.at[1, 0, 0, :, c], qg.at[2 - 2 * n, 0, 0, :, c], halo_s.at[n, 0], halo_r.at[1 - n, 0], beside[n]).start())

    def lend_queries(j, start, stop):
        for a in range(start, stop):
            await_bytes(qg.at[1, j, a], xin_r.at[j, a])
            each(lambda n: remote(qg.at[1, j, a], qg.at[2 - 2 * n, j, a], halo_s.at[n, j], halo_r.at[1 - n, j], beside[n]).start())

    def return_queries(j):
        each(lambda n: remote(dqs.at[j, 2 * n], dqr.at[j, 1 - n], dq_s.at[n, j], dq_r.at[1 - n, j], beside[n]).start())

    def return_half(half):
        rows = pl.ds(half * 2 * TILE, 2 * TILE)
        each(lambda n: remote(dqs.at[nh - 1, 2 * n, rows], dqr.at[nh - 1, 1 - n, rows], dqh_s.at[n, half], dqh_r.at[1 - n, half], beside[n]).start())

    def finish_half(half):
        j, rows = nh - 1, pl.ds(half * 2 * TILE, 2 * TILE)
        each(lambda n: await_bytes(dqr.at[j, n, rows], dqh_r.at[n, half]))
        total = dqf[j, rows] + dqr[j, 0, rows].astype(jnp.float32) + dqr[j, 1, rows].astype(jnp.float32)
        ost[j, 0, half] = total.astype(jnp.bfloat16).reshape(ost.shape[3:])
        to = oq_ref.at[0, 0, :, :, lanes(me, j)]

        def across(k):
            xk = lax.rem(x + k, 4)
            remote(ost.at[j, 0, half, :, xk], to, out_s.at[j, 0], out_r.at[0], (half, h, xk)).start()

        @pl.when(f == half)
        def _():
            pltpu.make_async_copy(ost.at[j, 0, half, :, x], to, out_r.at[0]).start()

        pl.when(f != half)(lambda: across(0))
        for k in range(1, 4):
            across(k)

    def finish_queries(j):
        each(lambda n: await_bytes(dqr.at[j, n], dq_r.at[n, j]))
        total = dqf[j] + dqr[j, 0].astype(jnp.float32) + dqr[j, 1].astype(jnp.float32)
        ost[j, 0] = total.astype(jnp.bfloat16).reshape(ost.shape[2:])
        leave(j, 0, oq_ref)

    def neighbours_of(action):
        def body(n, carry):
            ahead = jnp.where(n == 0, h - 1, h + 1)
            pl.when(jnp.logical_and(ahead >= 0, ahead < NROWS))(lambda: action(n, (f, ahead, x)))
            return carry

        lax.fori_loop(0, 2, body, 0)

    def weights_beside(j):
        def one(n, device):
            await_bytes(qg.at[2 * n, j], halo_r.at[n, j])
            phase_a(2 * n, j, lax.rem(j, 3), qg, kv, bias, es, dps, ms, pst)
            remote(pst.at[j, 2 * n], prc.at[j, 1 - n], part_s.at[n, j], part_r.at[1 - n, j], device).start()

        neighbours_of(one)

    def gradients(j):
        dka[...] = jnp.zeros_like(dka)
        dva[...] = jnp.zeros_like(dva)

        def one(n, device):
            await_bytes(fin.at[j, 2 * n], fin_r.at[n, j])
            phase_b(2 * n, j, lax.rem(j, 3), qg, kv, es, dps, ms, fin, dka, dva, dqs, dqf)

        neighbours_of(one)

        @pl.when(j == nh - 1)
        def _():
            return_half(0)
            return_half(1)

        phase_b(1, j, lax.rem(j, 3), qg, kv, es, dps, ms, fin, dka, dva, dqs, dqf)
        ost[j, 1] = (dka[...] * HD**-0.5).astype(jnp.bfloat16).reshape(ost.shape[2:])
        ost[j, 2] = dva[...].astype(jnp.bfloat16).reshape(ost.shape[2:])
        leave(j, 1, ok_ref)
        leave(j, 2, ov_ref)

    def step(t, carry):
        pl.when(t + 1 < nh)(lambda: lend_queries(t + 1, 0, 1))

        @pl.when(t >= nh - 2)
        def _():
            low = jnp.where(t < nh, t - nh + 2, t - 2)
            high = jnp.where(t == nh - 2, 1, t - 1)
            lax.fori_loop(low, high, lambda j, c: (gradients(j), c)[1], 0)

        @pl.when(jnp.logical_and(t >= 1, t < nh + 1))
        def _():
            j = t - 1
            each(lambda n: await_bytes(prc.at[j, n], part_r.at[n, j]))
            combine(j, pst, prc, fin)
            each(lambda n: remote(fin.at[j, 1], fin.at[j, 2 - 2 * n], fin_s.at[n, j], fin_r.at[1 - n, j], beside[n]).start())

        pl.when(t == nh - 1)(lambda: return_queries(1))
        pl.when(t + 1 < nh)(lambda: lend_queries(t + 1, 1, 2))

        @pl.when(t < nh)
        def _():
            for a in range(2):
                await_bytes(kv.at[t, a], xin_r.at[t, 2 + a])
            phase_a(1, t, lax.rem(t, 3), qg, kv, bias, es, dps, ms, pst)
            pl.when(t == 0)(lambda: each(lambda n: lend[n].wait_recv()))
            weights_beside(t)

        pl.when(t == nh - 2)(lambda: return_queries(0))
        pl.when(t == nh - 1)(lambda: return_queries(2))
        pl.when(t == nh)(lambda: return_queries(3))

        @pl.when(jnp.logical_or(t == nh - 1, t == nh))
        def _():
            lax.fori_loop(t - nh + 1, 2 * (t - nh) + 3, lambda j, c: (finish_queries(j), c)[1], 0)

        return carry

    near.wait()
    for n, dr in enumerate((1, 0, -1)):
        row = h + dr
        inside = jnp.logical_and(row >= 0, row < NROWS)
        for kt in range(4):
            wanted = jnp.where(inside, (kt // 2 * NROWS + row) * 2 + kt % 2, -2)
            for c in range(2):
                found = jnp.where(nb_ref[0, 0, c : c + 1, :] == wanted, 0.0, NONE)
                found = jnp.max(found, axis=-1, keepdims=True)
                tab[n, f, kt : kt + 1, c * TILE : (c + 1) * TILE] = jnp.broadcast_to(found, (1, TILE))
    swap = remote(tab.at[:, f], tab.at[:, f], tab_s, tab_r, (1 - f, h, x))
    swap.start()

    lend_first()
    lend_queries(0, 1, 2)
    swap.wait()
    for g in range(2):
        lent[:, 4 * g : 4 * g + 4, :] = tab[:, g]
    bias[1] = lent[1]
    lend = [remote(lent.at[2 * n], bias.at[2 * n], bias_s.at[n], bias_r.at[n], beside[1 - n]) for n in range(2)]
    each(lambda n: lend[1 - n].start())

    @pl.when(h == 0)
    def _():
        blank(0)

    @pl.when(h == NROWS - 1)
    def _():
        blank(1)

    lax.fori_loop(0, nh + 2, step, 0)
    finish_queries(3)
    finish_half(0)
    finish_half(1)

    each(lambda n: lend[1 - n].wait_send())

    def settle(j, carry):
        sent = dqs.at[j, 0, pl.ds(0, 7 * TILE // 2)]
        for a in range(4):
            await_bytes(sent, xin_s.at[j, a])
        for a in range(3):
            await_bytes(sent, out_s.at[j, a])

        def settle_beside(n):
            await_bytes(qg.at[1, j], halo_s.at[n, j])
            await_bytes(prc.at[j, n], part_s.at[n, j])
            await_bytes(prc.at[j, n], fin_s.at[n, j])
            pl.when(j < nh - 1)(lambda: await_bytes(dqr.at[j, n], dq_s.at[n, j]))

        each(settle_beside)
        return carry

    lax.fori_loop(0, nh, settle, 0)
    for half in range(2):
        each(lambda n: await_bytes(dqr.at[nh - 1, n, pl.ds(0, 2 * TILE)], dqh_s.at[n, half]))
    for a, out in enumerate((oq_ref, ok_ref, ov_ref)):
        await_bytes(out, out_r.at[a])


def hand_over(aq, ak, av, bq, bk, bv, out):
    copies = [pltpu.make_async_copy(a, b, out.at[n]) for n, (a, b) in enumerate(((aq, bq), (ak, bk), (av, bv)))]
    for copy in copies:
        copy.start()
    for copy in copies:
        copy.wait()


def local(queries, keys, values, out_grad, neighbours):
    nh = queries.shape[-1] // HD // 8
    tiles = (2, 2, 4, TILE // 4, HD)
    bf, f32 = jnp.bfloat16, jnp.float32
    dma = pltpu.SemaphoreType.DMA
    any_spec = pl.BlockSpec(memory_space=pl.ANY)
    shape = jax.ShapeDtypeStruct(queries.shape, bf)
    products = 5 * 512 * 1536 * HD * nh
    grads = pl.pallas_call(
        functools.partial(kernel, nh),
        out_shape=(pltpu.VMEM(queries.shape, bf),) * 3,
        in_specs=[any_spec] * 5,
        out_specs=[pl.BlockSpec(memory_space=pltpu.VMEM)] * 3,
        scratch_shapes=[
            pltpu.VMEM(neighbours.shape, jnp.int32),
            pltpu.VMEM((3, nh, 2) + tiles, bf),
            pltpu.VMEM((nh, 2) + tiles, bf),
            pltpu.VMEM((3, 2, 4, 256), f32),
            pltpu.VMEM((3, 8, 256), f32),
            pltpu.VMEM((3, 8, 256), f32),
            pltpu.VMEM((3, 6, 4, TILE, 256), f32),
            pltpu.VMEM((3, 6, 4, TILE, 256), f32),
            pltpu.VMEM((3, 6, 8, 256), f32),
            pltpu.VMEM((nh, 3, 4, 256), f32),
            pltpu.VMEM((nh, 2, 4, 256), f32),
            pltpu.VMEM((nh, 3, 4, 256), f32),
            pltpu.VMEM((4, TILE, HD), f32),
            pltpu.VMEM((4, TILE, HD), f32),
            pltpu.VMEM((nh, 3, 512, HD), bf),
            pltpu.VMEM((nh, 2, 512, HD), bf),
            pltpu.VMEM((nh, 512, HD), f32),
            pltpu.VMEM((nh, 3) + tiles, bf),
            dma((nh, 4)), dma((nh, 4)),
            dma((2, nh)), dma((2, nh)),
            dma((2, nh)), dma((2, nh)),
            dma((2, nh)), dma((2, nh)),
            dma((2, nh)), dma((2, nh)),
            dma((nh, 3)), dma((3,)),
            dma(()), dma(()),
            dma((2,)), dma((2,)),
            dma(()),
            dma((2, 2)), dma((2, 2)),
            dma(()),
        ],
        compiler_params=pltpu.CompilerParams(
            collective_id=0, has_side_effects=True, vmem_limit_bytes=48 * 1024 * 1024
        ),
        cost_estimate=pl.CostEstimate(
            flops=2 * products, bytes_accessed=7 * 2 * queries.size, transcendentals=512 * 1536 * nh
        ),
        name="window_backward",
    )(*(pltpu.with_memory_space_constraint(a, pltpu.HBM) for a in (queries, keys, values, out_grad, neighbours)))
    return pl.pallas_call(
        hand_over,
        out_shape=(shape, shape, shape),
        in_specs=[pl.BlockSpec(memory_space=pltpu.VMEM)] * 3,
        out_specs=[any_spec] * 3,
        scratch_shapes=[dma((3,))],
        name="hand_over",
    )(*(pltpu.with_memory_space_constraint(a, pltpu.VMEM) for a in grads))


def solution(mesh):
    whole = P("frames", "rows", None, "heads", None)
    return jax.shard_map(
        local,
        mesh=mesh,
        in_specs=(whole, whole, whole, whole, P("frames", "rows", None, None)),
        out_specs=(whole, whole, whole),
        check_vma=False,
    )
```

```python
import functools

import jax
import jax.numpy as jnp
from jax import lax
from jax.experimental import pallas as pl
from jax.experimental.pallas import tpu as pltpu
from jax.sharding import PartitionSpec as P

MESH = pl.DeviceIdType.MESH
HD = 128
TILE = 128
NROWS = 16
LOG2E = 1.4426950408889634
NONE = -1e30
NT = (((1,), (1,)), ((), ()))
NN = (((1,), (0,)), ((), ()))
TN = (((0,), (0,)), ((), ()))


def dot(a, b, dims):
    return lax.dot_general(a, b, dims, preferred_element_type=jnp.float32)


def phase_a(s, j, p, qg, kv, bias, es, dps, ms, pst):
    scale = LOG2E * HD**-0.5

    def block(f, carry):
        i = 2 * s + f
        q = qg[s, j, 0, f].reshape(2 * TILE, HD)
        g = qg[s, j, 1, f].reshape(2 * TILE, HD)
        peaks, sums, prods = [], [], []
        for kt in range(4):
            k = kv[j, 0, kt // 2, kt % 2].reshape(TILE, HD)
            v = kv[j, 1, kt // 2, kt % 2].reshape(TILE, HD)
            st = dot(k, q, NT) * scale
            m = jnp.max(st, axis=0, keepdims=True)
            e = jnp.exp2(st - m)
            dp = dot(v, g, NT)
            es[p, i, kt] = e
            dps[p, i, kt] = dp
            mb = m + bias[s, 4 * f + kt : 4 * f + kt + 1, :]
            ms[p, i, kt : kt + 1, :] = mb
            peaks.append(mb)
            sums.append(jnp.sum(e, axis=0, keepdims=True))
            prods.append(jnp.sum(e * dp, axis=0, keepdims=True))
        top = functools.reduce(jnp.maximum, peaks)
        ws = [jnp.exp2(mb - top) for mb in peaks]
        total = sum(w * l for w, l in zip(ws, sums))
        pst[j, s, 2 * f : 2 * f + 1, :] = top + jnp.log2(total)
        pst[j, s, 2 * f + 1 : 2 * f + 2, :] = sum(w * d for w, d in zip(ws, prods)) / total
        return carry

    block(0, 0)
    block(1, 0)


def combine(j, pst, prc, fin):
    for f in range(2):
        rows = slice(2 * f, 2 * f + 2)
        parts = [pst[j, 1, rows], prc[j, 0, rows], prc[j, 1, rows]]
        top = functools.reduce(jnp.maximum, [x[0:1] for x in parts])
        ws = [jnp.exp2(x[0:1] - top) for x in parts]
        total = sum(ws)
        prod = sum(w * x[1:2] for w, x in zip(ws, parts))
        fin[j, 1, 2 * f : 2 * f + 1, :] = top + jnp.log2(total)
        fin[j, 1, 2 * f + 1 : 2 * f + 2, :] = prod / total


def phase_b(s, j, p, qg, kv, es, dps, ms, fin, dka, dva, dqs, dqf):
    scale = HD**-0.5

    def block(f, carry):
        i = 2 * s + f
        q = qg[s, j, 0, f].reshape(2 * TILE, HD)
        g = qg[s, j, 1, f].reshape(2 * TILE, HD)
        lse = fin[j, s, 2 * f : 2 * f + 1, :]
        delta = fin[j, s, 2 * f + 1 : 2 * f + 2, :]
        probs, grads = [], []
        for kt in range(4):
            r = jnp.exp2(ms[p, i, kt : kt + 1, :] - lse)
            prob = es[p, i, kt] * r
            ds = (prob * (dps[p, i, kt] - delta)).astype(jnp.bfloat16)
            probs.append(prob.astype(jnp.bfloat16))
            grads.append(ds)
        probs, grads = jnp.concatenate(probs), jnp.concatenate(grads)
        dva[...] += dot(probs, g, NN).reshape(dva.shape)
        dka[...] += dot(grads, q, NN).reshape(dka.shape)
        dq = dot(kv[j, 0].reshape(4 * TILE, HD), grads, TN).T * scale
        rows = pl.ds(pl.multiple_of(f * 2 * TILE, 2 * TILE), 2 * TILE)
        if isinstance(s, int):
            dqf[j, rows] = dq
        else:
            dqs[j, s, rows] = dq.astype(jnp.bfloat16)
        return carry

    block(0, 0)
    block(1, 0)


def kernel(nh, q_ref, k_ref, v_ref, g_ref, nb_hbm, oq_ref, ok_ref, ov_ref,
           nb_ref, qg, kv, tab, lent, bias, es, dps, ms, pst, prc, fin, dka, dva, dqs, dqr, dqf, ost,
           xin_s, xin_r, halo_s, halo_r, part_s, part_r, fin_s, fin_r, dq_s, dq_r, out_s, out_r,
           tab_s, tab_r, bias_s, bias_r, nb_s, dqh_s, dqh_r, early_r):
    f = lax.axis_index("frames")
    h = lax.axis_index("rows")
    x = lax.axis_index("heads")
    me = x * 2 + f
    beside = (f, jnp.maximum(h - 1, 0), x), (f, jnp.minimum(h + 1, NROWS - 1), x)
    held = h > 0, h < NROWS - 1

    def member(k):
        across, other_core = ((1, 0), (3, 0), (2, 0), (1, 1), (3, 1), (2, 1), (0, 1))[k - 1]
        peer, core = lax.rem(x + across, 4), lax.rem(f + other_core, 2)
        return peer * 2 + core, (core, h, peer)

    barrier = pltpu.get_barrier_semaphore()
    for k in range(1, 8):
        pl.semaphore_signal(barrier, inc=1, device_id=member(k)[1], device_id_type=MESH)
    for n in range(2):

        @pl.when(held[n])
        def _():
            pl.semaphore_signal(barrier, inc=1, device_id=beside[n], device_id_type=MESH)

    near = pltpu.make_async_copy(nb_hbm, nb_ref, nb_s)
    near.start()
    pl.semaphore_wait(barrier, 7 + held[0].astype(jnp.int32) + held[1].astype(jnp.int32))

    def remote(src, dst, send, recv, device):
        return pltpu.make_async_remote_copy(
            src_ref=src, dst_ref=dst, send_sem=send, recv_sem=recv, device_id=device, device_id_type=MESH
        )

    def await_bytes(ref, sem):
        pltpu.make_async_copy(ref, ref, sem).wait()

    def each(action):
        for n in range(2):
            pl.when(held[n])(functools.partial(action, n))

    def lanes(owner, j):
        return pl.ds(pl.multiple_of((owner * nh + j) * HD, HD), HD)

    def enter(j, pair, skip=0):
        sides = ((q_ref, qg.at[1, j, 0]), (g_ref, qg.at[1, j, 1])), ((k_ref, kv.at[j, 0]), (v_ref, kv.at[j, 1]))
        for a, (src, dst) in list(enumerate(sides[pair]))[skip:]:
            to = dst.at[f, :, x]
            recv = xin_r.at[j, 2 * pair + a]
            pltpu.make_async_copy(src.at[0, 0, :, :, lanes(me, j)], to, recv).start()
            for k in range(1, 8):
                other, device = member(k)
                remote(src.at[0, 0, :, :, lanes(other, j)], to, xin_s.at[j, 2 * pair + a], recv, device).start()

    def enter_first():
        for c in range(2):
            to = qg.at[1, 0, 0, f, c, x]
            recv = xin_r.at[0, 0] if c else early_r
            pltpu.make_async_copy(q_ref.at[0, 0, c, :, lanes(me, 0)], to, recv).start()
            for k in range(1, 8):
                other, device = member(k)
                remote(q_ref.at[0, 0, c, :, lanes(other, 0)], to, xin_s.at[0, 0], recv, device).start()

    def leave(j, a, out):
        to = out.at[0, 0, :, :, lanes(me, j)]
        pltpu.make_async_copy(ost.at[j, a, f, :, x], to, out_r.at[a]).start()
        for k in range(1, 8):
            other, device = member(k)
            remote(ost.at[j, a, other % 2, :, other // 2], to, out_s.at[j, a], out_r.at[a], device).start()

    def blank(n):
        dqr[:, n] = jnp.zeros_like(dqr[:, n])
        prc[:, n] = jnp.full_like(prc[:, n], NONE)

    def enter_both(j, carry):
        pl.when(j < nh)(lambda: enter(j, 0))
        pl.when(j >= 1)(lambda: enter(j - 1, 1))
        return carry

    enter_first()
    enter(0, 0, 1)
    lax.fori_loop(1, nh + 1, enter_both, 0)

    def lend_first():
        for c in range(2):
            await_bytes(qg.at[1, 0, 0, :, c], xin_r.at[0, 0] if c else early_r)
            each(lambda n: remote(qg.at[1, 0, 0, :, c], qg.at[2 - 2 * n, 0, 0, :, c], halo_s.at[n, 0], halo_r.at[1 - n, 0], beside[n]).start())

    def lend_queries(j, start, stop):
        for a in range(start, stop):
            await_bytes(qg.at[1, j, a], xin_r.at[j, a])
            each(lambda n: remote(qg.at[1, j, a], qg.at[2 - 2 * n, j, a], halo_s.at[n, j], halo_r.at[1 - n, j], beside[n]).start())

    def return_queries(j):
        each(lambda n: remote(dqs.at[j, 2 * n], dqr.at[j, 1 - n], dq_s.at[n, j], dq_r.at[1 - n, j], beside[n]).start())

    def return_half(half):
        rows = pl.ds(half * 2 * TILE, 2 * TILE)
        each(lambda n: remote(dqs.at[nh - 1, 2 * n, rows], dqr.at[nh - 1, 1 - n, rows], dqh_s.at[n, half], dqh_r.at[1 - n, half], beside[n]).start())

    def finish_half(half):
        j, rows = nh - 1, pl.ds(half * 2 * TILE, 2 * TILE)
        each(lambda n: await_bytes(dqr.at[j, n, rows], dqh_r.at[n, half]))
        total = dqf[j, rows] + dqr[j, 0, rows].astype(jnp.float32) + dqr[j, 1, rows].astype(jnp.float32)
        ost[j, 0, half] = total.astype(jnp.bfloat16).reshape(ost.shape[3:])
        to = oq_ref.at[0, 0, :, :, lanes(me, j)]

        def across(k):
            xk = lax.rem(x + k, 4)
            remote(ost.at[j, 0, half, :, xk], to, out_s.at[j, 0], out_r.at[0], (half, h, xk)).start()

        @pl.when(f == half)
        def _():
            pltpu.make_async_copy(ost.at[j, 0, half, :, x], to, out_r.at[0]).start()

        pl.when(f != half)(lambda: across(0))
        for k in range(1, 4):
            across(k)

    def finish_queries(j):
        each(lambda n: await_bytes(dqr.at[j, n], dq_r.at[n, j]))
        total = dqf[j] + dqr[j, 0].astype(jnp.float32) + dqr[j, 1].astype(jnp.float32)
        ost[j, 0] = total.astype(jnp.bfloat16).reshape(ost.shape[2:])
        leave(j, 0, oq_ref)

    def neighbours_of(action):
        def body(n, carry):
            ahead = jnp.where(n == 0, h - 1, h + 1)
            pl.when(jnp.logical_and(ahead >= 0, ahead < NROWS))(lambda: action(n, (f, ahead, x)))
            return carry

        lax.fori_loop(0, 2, body, 0)

    def weights_beside(j):
        def one(n, device):
            await_bytes(qg.at[2 * n, j], halo_r.at[n, j])
            phase_a(2 * n, j, lax.rem(j, 3), qg, kv, bias, es, dps, ms, pst)
            remote(pst.at[j, 2 * n], prc.at[j, 1 - n], part_s.at[n, j], part_r.at[1 - n, j], device).start()

        neighbours_of(one)

    def gradients(j):
        dka[...] = jnp.zeros_like(dka)
        dva[...] = jnp.zeros_like(dva)

        def one(n, device):
            await_bytes(fin.at[j, 2 * n], fin_r.at[n, j])
            phase_b(2 * n, j, lax.rem(j, 3), qg, kv, es, dps, ms, fin, dka, dva, dqs, dqf)

        neighbours_of(one)

        @pl.when(j == nh - 1)
        def _():
            return_half(0)
            return_half(1)

        phase_b(1, j, lax.rem(j, 3), qg, kv, es, dps, ms, fin, dka, dva, dqs, dqf)
        ost[j, 1] = (dka[...] * HD**-0.5).astype(jnp.bfloat16).reshape(ost.shape[2:])
        ost[j, 2] = dva[...].astype(jnp.bfloat16).reshape(ost.shape[2:])
        leave(j, 1, ok_ref)
        leave(j, 2, ov_ref)

    def step(t, carry):
        pl.when(t + 1 < nh)(lambda: lend_queries(t + 1, 0, 1))

        @pl.when(t >= nh - 2)
        def _():
            low = jnp.where(t < nh, t - nh + 2, t - 2)
            high = jnp.where(t == nh - 2, 1, t - 1)
            lax.fori_loop(low, high, lambda j, c: (gradients(j), c)[1], 0)

        @pl.when(t < nh)
        def _():
            for a in range(2):
                await_bytes(kv.at[t, a], xin_r.at[t, 2 + a])
            phase_a(1, t, lax.rem(t, 3), qg, kv, bias, es, dps, ms, pst)

        @pl.when(jnp.logical_and(t >= 1, t < nh + 1))
        def _():
            j = t - 1
            each(lambda n: await_bytes(prc.at[j, n], part_r.at[n, j]))
            combine(j, pst, prc, fin)
            each(lambda n: remote(fin.at[j, 1], fin.at[j, 2 - 2 * n], fin_s.at[n, j], fin_r.at[1 - n, j], beside[n]).start())

        pl.when(t == nh - 1)(lambda: return_queries(1))
        pl.when(t + 1 < nh)(lambda: lend_queries(t + 1, 1, 2))

        @pl.when(t < nh)
        def _():
            pl.when(t == 0)(lambda: each(lambda n: lend[n].wait_recv()))
            weights_beside(t)

        pl.when(t == nh - 2)(lambda: return_queries(0))
        pl.when(t == nh - 1)(lambda: return_queries(2))
        pl.when(t == nh)(lambda: return_queries(3))

        @pl.when(jnp.logical_or(t == nh - 1, t == nh))
        def _():
            lax.fori_loop(t - nh + 1, 2 * (t - nh) + 3, lambda j, c: (finish_queries(j), c)[1], 0)

        return carry

    near.wait()
    for n, dr in enumerate((1, 0, -1)):
        row = h + dr
        inside = jnp.logical_and(row >= 0, row < NROWS)
        for kt in range(4):
            wanted = jnp.where(inside, (kt // 2 * NROWS + row) * 2 + kt % 2, -2)
            for c in range(2):
                found = jnp.where(nb_ref[0, 0, c : c + 1, :] == wanted, 0.0, NONE)
                found = jnp.max(found, axis=-1, keepdims=True)
                tab[n, f, kt : kt + 1, c * TILE : (c + 1) * TILE] = jnp.broadcast_to(found, (1, TILE))
    swap = remote(tab.at[:, f], tab.at[:, f], tab_s, tab_r, (1 - f, h, x))
    swap.start()

    lend_first()
    lend_queries(0, 1, 2)
    swap.wait()
    for g in range(2):
        lent[:, 4 * g : 4 * g + 4, :] = tab[:, g]
    bias[1] = lent[1]
    lend = [remote(lent.at[2 * n], bias.at[2 * n], bias_s.at[n], bias_r.at[n], beside[1 - n]) for n in range(2)]
    each(lambda n: lend[1 - n].start())

    @pl.when(h == 0)
    def _():
        blank(0)

    @pl.when(h == NROWS - 1)
    def _():
        blank(1)

    lax.fori_loop(0, nh + 2, step, 0)
    finish_queries(3)
    finish_half(0)
    finish_half(1)

    each(lambda n: lend[1 - n].wait_send())

    def settle(j, carry):
        sent = dqs.at[j, 0, pl.ds(0, 7 * TILE // 2)]
        for a in range(4):
            await_bytes(sent, xin_s.at[j, a])
        for a in range(3):
            await_bytes(sent, out_s.at[j, a])

        def settle_beside(n):
            await_bytes(qg.at[1, j], halo_s.at[n, j])
            await_bytes(prc.at[j, n], part_s.at[n, j])
            await_bytes(prc.at[j, n], fin_s.at[n, j])
            pl.when(j < nh - 1)(lambda: await_bytes(dqr.at[j, n], dq_s.at[n, j]))

        each(settle_beside)
        return carry

    lax.fori_loop(0, nh, settle, 0)
    for half in range(2):
        each(lambda n: await_bytes(dqr.at[nh - 1, n, pl.ds(0, 2 * TILE)], dqh_s.at[n, half]))
    for a, out in enumerate((oq_ref, ok_ref, ov_ref)):
        await_bytes(out, out_r.at[a])


def hand_over(aq, ak, av, bq, bk, bv, out):
    copies = [pltpu.make_async_copy(a, b, out.at[n]) for n, (a, b) in enumerate(((aq, bq), (ak, bk), (av, bv)))]
    for copy in copies:
        copy.start()
    for copy in copies:
        copy.wait()


def local(queries, keys, values, out_grad, neighbours):
    nh = queries.shape[-1] // HD // 8
    tiles = (2, 2, 4, TILE // 4, HD)
    bf, f32 = jnp.bfloat16, jnp.float32
    dma = pltpu.SemaphoreType.DMA
    any_spec = pl.BlockSpec(memory_space=pl.ANY)
    shape = jax.ShapeDtypeStruct(queries.shape, bf)
    products = 5 * 512 * 1536 * HD * nh
    grads = pl.pallas_call(
        functools.partial(kernel, nh),
        out_shape=(pltpu.VMEM(queries.shape, bf),) * 3,
        in_specs=[any_spec] * 5,
        out_specs=[pl.BlockSpec(memory_space=pltpu.VMEM)] * 3,
        scratch_shapes=[
            pltpu.VMEM(neighbours.shape, jnp.int32),
            pltpu.VMEM((3, nh, 2) + tiles, bf),
            pltpu.VMEM((nh, 2) + tiles, bf),
            pltpu.VMEM((3, 2, 4, 256), f32),
            pltpu.VMEM((3, 8, 256), f32),
            pltpu.VMEM((3, 8, 256), f32),
            pltpu.VMEM((3, 6, 4, TILE, 256), f32),
            pltpu.VMEM((3, 6, 4, TILE, 256), f32),
            pltpu.VMEM((3, 6, 8, 256), f32),
            pltpu.VMEM((nh, 3, 4, 256), f32),
            pltpu.VMEM((nh, 2, 4, 256), f32),
            pltpu.VMEM((nh, 3, 4, 256), f32),
            pltpu.VMEM((4, TILE, HD), f32),
            pltpu.VMEM((4, TILE, HD), f32),
            pltpu.VMEM((nh, 3, 512, HD), bf),
            pltpu.VMEM((nh, 2, 512, HD), bf),
            pltpu.VMEM((nh, 512, HD), f32),
            pltpu.VMEM((nh, 3) + tiles, bf),
            dma((nh, 4)), dma((nh, 4)),
            dma((2, nh)), dma((2, nh)),
            dma((2, nh)), dma((2, nh)),
            dma((2, nh)), dma((2, nh)),
            dma((2, nh)), dma((2, nh)),
            dma((nh, 3)), dma((3,)),
            dma(()), dma(()),
            dma((2,)), dma((2,)),
            dma(()),
            dma((2, 2)), dma((2, 2)),
            dma(()),
        ],
        compiler_params=pltpu.CompilerParams(
            collective_id=0, has_side_effects=True, vmem_limit_bytes=48 * 1024 * 1024
        ),
        cost_estimate=pl.CostEstimate(
            flops=2 * products, bytes_accessed=7 * 2 * queries.size, transcendentals=512 * 1536 * nh
        ),
        name="window_backward",
    )(*(pltpu.with_memory_space_constraint(a, pltpu.HBM) for a in (queries, keys, values, out_grad, neighbours)))
    return pl.pallas_call(
        hand_over,
        out_shape=(shape, shape, shape),
        in_specs=[pl.BlockSpec(memory_space=pltpu.VMEM)] * 3,
        out_specs=[any_spec] * 3,
        scratch_shapes=[dma((3,))],
        name="hand_over",
    )(*(pltpu.with_memory_space_constraint(a, pltpu.VMEM) for a in grads))


def solution(mesh):
    whole = P("frames", "rows", None, "heads", None)
    return jax.shard_map(
        local,
        mesh=mesh,
        in_specs=(whole, whole, whole, whole, P("frames", "rows", None, None)),
        out_specs=(whole, whole, whole),
        check_vma=False,
    )
```
